512 devices in a mesh: sec: 128 (over y, z, core), tile: 4 (over x).
Axes of the slice: x: 4, y: 4, z: 16, core: 2. Of those that a mesh axis runs over, the one named last changes fastest.
Arguments:
- node_flow: float32 [128, 2, 256, 512], P('sec', None, 'tile'), may hold values from -6 to 6
- classes: int32 [128, 256, 512], P('sec', 'tile'), may hold values from 0 to 7
- table: float32 [8], replicated, may hold values from 0.3 to 2.5
- z_couple: float32 [128], replicated, may hold values from 22 to 30
- match_dest: int32 [131072, 1], P(('sec', 'tile')), may hold values from 0 to 127; in each aligned block of 256 rows (0 to 255, 256 to 511, ...) at most 4 rows name the same one
- match_slot: int32 [131072], P(('sec', 'tile')), may hold values from 0 to 255
- match_vectors: float32 [131072, 256], P(('sec', 'tile')), may hold values from -6 to 6
Outputs:
- aligned: float32 [128, 2, 256, 512], P('sec', None, 'tile')
The draws below stay inside these ranges and needn't reach their ends.
Inputs may be any that keep to these rules, and one draw needn't show every extreme that they name: `match_dest`: among the 256 rows of one device no value occurs more than 4 times; one value occurs exactly 4 times.
All inputs are finite; a program needn't handle non-finite values.
Results may differ from the reference program's by a relative error of at most 0.00026.
Values sent between devices are 32-bit elements; how exact they have to be, the bound alone decides.
A program may use at most 192 MiB of HBM per device.

```python
import math
import jax
import jax.numpy as jnp
import numpy as np
from jax import lax

W = 512
TILE = 128
SEC_DEV = 1
ROWS_DEV = 64
NCLASS = 8
ROUNDS = 2
ISTEPS = 2
H = 256
SECTIONS = 128
MATCH_DEV = 256
CAP = 4
MATCHES = 131072
TILES_DEV = 256
N_SEC = 128
N_TILE = 4


def draw_node_flow(key, part):
    key = jax.random.fold_in(key, 11)
    common_key, noise_key = jax.random.split(key, 2)
    common = jax.random.normal(common_key, (2, H, W), jnp.float32)
    noise = jax.random.normal(noise_key, (SECTIONS, 2, H, W), jnp.float32)
    field = common[None] + 0.6 * noise
    return jnp.clip(field, -6.0, 6.0)


def draw_z_couple(key, part):
    key = jax.random.fold_in(key, 12)
    values = jax.random.uniform(key, (SECTIONS,), jnp.float32, 22.0, 30.0)
    return values


def set_ends(values, rng, low, high):
    place = [jax.random.randint(jax.random.fold_in(rng, axis), (), 0, length) for axis, length in enumerate(values.shape)]
    longest = values.shape.index(max(values.shape))
    beside = place[:longest] + [(place[longest] + 1) % values.shape[longest]] + place[longest + 1:]
    return values.at[tuple(place)].set(low).at[tuple(beside)].set(high)


def level_of(rng, dims, cuts, low, top_value):
    def one(position, parts):
        steps = jax.random.uniform(jax.random.fold_in(jax.random.fold_in(rng, 6), position), (parts,), jnp.float32, low / len(cuts), top_value / len(cuts))
        return jnp.repeat(jnp.exp(steps), dims[position] // parts).reshape((-1,) + (1,) * (len(dims) - position - 1))

    loudness = one(*cuts[0])
    for cut in cuts[1:]:
        loudness = loudness * one(*cut)
    return loudness


def shared_out(rng, own, number, rows, amount, top, most, lean):
    order = jax.random.permutation(rng, amount)
    heavy_load, ordinary = shares(amount, rows * top, most, lean, True), shares(amount, rows * top, most, lean, False)
    places = jnp.arange(amount)

    def named(tallies, turn):
        used = int((tallies > 0).sum())
        fixed = max(1, used // 4)
        shifted = fixed + (places - fixed + turn * (used - fixed)) % max(1, amount - fixed)
        return jnp.zeros((amount,), jnp.int32).at[order[jnp.where(places < fixed, places, shifted)]].set(jnp.asarray(tallies, jnp.int32))

    tallies = jnp.where(number % 4 == 0, named(heavy_load, number // 4), named(ordinary, number - number // 4 - 1))
    mixed = jax.random.permutation(jax.random.fold_in(own, 3), amount)
    giver, receiver = mixed[0:amount // 2 * 2:2], mixed[1:amount // 2 * 2:2]
    margin = jnp.minimum(tallies[giver] - 1, most - tallies[receiver]) // 2
    margin = jnp.where((giver == order[0]) | (receiver == order[0]) | (tallies[receiver] == 0), 0, jnp.maximum(margin, 0))
    shifted = jax.random.randint(jax.random.fold_in(own, 4), (amount // 2,), 0, 1 << 20) % (margin + 1)
    tallies = tallies.at[giver].add(-shifted).at[receiver].add(shifted)
    members = jnp.searchsorted(jnp.cumsum(tallies), jnp.arange(rows * top), side="right").astype(jnp.int32)
    table = members.reshape(top, rows).T
    table = table[jax.random.permutation(jax.random.fold_in(own, 1), rows)]
    turn = jax.random.randint(jax.random.fold_in(own, 2), (rows, 1), 0, top)
    return jnp.take_along_axis(table, (jnp.arange(top)[None, :] + turn) % top, axis=1)


def shares(number_of, total, most, slope, full):
    portions = [(1 << 20) // math.isqrt(grade ** slope) + 1 for grade in range(1, number_of + 1)]
    largest = most if full else min(most, max(-(-total // number_of), total * portions[0] // sum(portions)))
    least = 1 if total - largest >= number_of - 1 else 0
    holding, rest = [largest] + [least] * (number_of - 1), total - largest - least * (number_of - 1)
    while rest > 0:
        candidates = [i for i in range(1, number_of) if holding[i] < largest] or [i for i in range(1, number_of) if holding[i] < most]
        pool, budget = sum([portions[i] for i in candidates]), rest
        for i in candidates:
            addition = min(most - holding[i], max(1, budget * portions[i] // pool), rest)
            holding[i] = holding[i] + addition
            rest = rest - addition
    return np.array(holding)


def centred(stream_key, shape, spread, reach, pieces=(), kind=jnp.bfloat16):
    gain = level_of(stream_key, shape, pieces, -0.22, 0.18) if pieces else 1.0
    entries = jax.random.normal(stream_key, shape, jnp.float32) * spread * gain
    return jnp.minimum(jnp.maximum(entries, -reach), reach).astype(kind)


def setup_inputs(seed: int = 0) -> dict:
    key_list = jax.random.split(jax.random.key(seed), 8)
    node_flow = draw_node_flow(jax.random.fold_in(key_list[7], 71), 0)
    classes = set_ends(jax.random.randint(key_list[1], (SECTIONS, H, W), 0, NCLASS), jax.random.fold_in(key_list[1], 1), 0, NCLASS - 1).astype(jnp.int32)
    table = jnp.clip(jnp.exp(jax.random.uniform(key_list[2], (NCLASS,), jnp.float32, math.log(0.3), math.log(2.5))), 0.3, 2.5)
    z_couple = draw_z_couple(jax.random.fold_in(key_list[7], 71), 0)
    match_dest_keys = jax.random.split(jax.random.fold_in(key_list[4], 1), MATCHES // MATCH_DEV)
    match_dest_turns = jax.random.permutation(jax.random.fold_in(key_list[4], 3), MATCHES // MATCH_DEV)
    match_dest = jax.vmap(lambda own, number: shared_out(jax.random.fold_in(key_list[4], 2), own, number, MATCH_DEV, N_SEC, 1, CAP, 1))(match_dest_keys, match_dest_turns).reshape((MATCHES, 1))
    match_slot = set_ends(jax.random.randint(key_list[5], (MATCHES,), 0, SEC_DEV * TILES_DEV), jax.random.fold_in(key_list[5], 1), 0, (SEC_DEV * TILES_DEV) - 1).astype(jnp.int32)
    match_vectors = centred(key_list[6], (MATCHES, 2 * TILE), 1.0, 6.0, ((0, 512),), jnp.float32)
    return dict(node_flow=node_flow, classes=classes, table=table, z_couple=z_couple, match_dest=match_dest, match_slot=match_slot, match_vectors=match_vectors)


relax_rate = 0.05

def stiffness_map(classes, table):
    result = jnp.zeros(classes.shape, table.dtype)
    for level in range(NCLASS):
        result = result + jnp.where(classes == level, table[level], jnp.zeros((), table.dtype))
    return result

def band_coefs(z_couple):
    before = jnp.concatenate([jnp.zeros((1,), z_couple.dtype), z_couple[:-1]])
    lower = -before
    diagonal = 1.0 + z_couple + before
    upper = jnp.concatenate([-z_couple[:-1], jnp.zeros((1,), z_couple.dtype)])
    return (lower, diagonal, upper)

def plane_step(field, stiffness, pulled, counts):
    padded = jnp.pad(field, ((0, 0), (0, 0), (1, 1), (1, 1)))
    laplace = padded[:, :, 2:, 1:-1] + padded[:, :, :-2, 1:-1] + padded[:, :, 1:-1, 2:] + padded[:, :, 1:-1, :-2] - 4.0 * field
    return field + relax_rate * (stiffness[:, None] * laplace + (pulled - counts[:, None] * field))

def reference(node_flow, classes, table, z_couple, match_dest, match_slot, match_vectors):
    sections, comps, rows, width = node_flow.shape
    per_row = width // TILE
    index = jnp.arange(MATCHES, dtype=jnp.int32)
    tile_index = index // MATCH_DEV % N_TILE
    section = match_dest[:, 0] * SEC_DEV + match_slot // TILES_DEV
    local_tile = match_slot % TILES_DEV
    row_index = tile_index * ROWS_DEV + local_tile // per_row
    target = ((section * rows + row_index) * per_row + local_tile % per_row).astype(jnp.int32)
    total = sections * rows * per_row
    pulled = jax.ops.segment_sum(match_vectors, target, total)
    pulled = pulled.reshape(sections, rows, per_row, comps, TILE).transpose(0, 3, 1, 2, 4).reshape(sections, comps, rows, width)
    counts = jax.ops.segment_sum(jnp.ones((MATCHES,), match_vectors.dtype), target, total)
    counts = jnp.repeat(counts.reshape(sections, rows, per_row), TILE, axis=2)
    stiffness = stiffness_map(classes, table)
    lower, diagonal, upper = band_coefs(z_couple)
    field = node_flow
    for cycle in range(ROUNDS):
        field = lax.linalg.tridiagonal_solve(lower, diagonal, upper, field.reshape(sections, -1)).reshape(field.shape)
        for step in range(ISTEPS):
            field = plane_step(field, stiffness, pulled, counts)
    return field
```

```python
import functools

import jax
import jax.numpy as jnp
from jax import lax
from jax.experimental import pallas as pl
from jax.experimental.pallas import tpu as pltpu
from jax.sharding import PartitionSpec as P

MESH = pl.DeviceIdType.MESH
RELAX = 0.05
CAP = 4
F32 = jnp.float32
BF16 = jnp.bfloat16


def iota(shape, dim):
    return lax.broadcasted_iota(jnp.int32, shape, dim)


def split3(v):
    hi = v.astype(BF16)
    rest = v - hi.astype(F32)
    mid = rest.astype(BF16)
    lo = (rest - mid.astype(F32)).astype(BF16)
    return hi, mid, lo


def inverse_parts(z, n):
    lanes = z.shape[1]
    lane = iota(z.shape, 1)
    w = 1.0 / z
    one = jnp.ones_like(z)
    m = (one, w, one, 1.0 + w)
    step = 1
    while step < n:
        first = lane < step
        b = [jnp.where(first, float(k in (0, 3)), pltpu.roll(v, step, 1)) for k, v in enumerate(m)]
        a = m
        m = (
            a[0] * b[0] + a[1] * b[2],
            a[0] * b[1] + a[1] * b[3],
            a[2] * b[0] + a[3] * b[2],
            a[2] * b[1] + a[3] * b[3],
        )
        step *= 2
    p_next = m[0] + m[1]
    p = jnp.where(lane == 0, 1.0, pltpu.roll(p_next, 1, 1))
    t = jnp.where(lane < n, 1.0 / (z * p * p_next), 0.0)
    p, t = p[:1], t[:1]
    r, c = iota((lanes, lanes), 0), iota((lanes, lanes), 1)
    p_col = jnp.sum(jnp.where(r == c, p, 0.0), axis=1, keepdims=True)
    t_col = jnp.sum(jnp.where(r == c, t, 0.0), axis=1, keepdims=True)
    tail_col = jnp.sum(jnp.where(c >= r, t, 0.0), axis=1, keepdims=True)
    tail = jnp.sum(jnp.where(r >= c, t_col, 0.0), axis=0, keepdims=True)
    return p, tail, p_col, tail_col


def kernel(
    dims,
    node_ref, classes_ref, table_ref, z_ref, dest_ref, slot_ref, vec_ref, out_ref,
    fin, xs, ext, fld, pq_send, pq_recv, lhs, cols,
    ma_send, ma_recv, mb_recv, sa_send, sa_recv, sb_send, sb_recv,
    halo_send, halo_recv, coef, cls, vec,
    load_sem, fin_send_sem, fin_recv_sem, pq_send_sem, pq_recv_sem, out_send_sem, out_recv_sem,
    ma_send_sem, ma_recv_sem, sa_send_sem, sa_recv_sem,
    mb_send_sem, mb_recv_sem, sb_send_sem, sb_recv_sem, halo_send_sem, halo_recv_sem,
):
    n_y, line, n_tile, rows, width = dims
    n_sec = n_y * line
    per_row = width // 128
    sec, t = lax.axis_index("sec"), lax.axis_index("tile")
    y, i = sec // line, sec % line
    tops = rows // 8

    def at_line(j):
        return (y * line + j, t)

    def at_y(q):
        return (q * line + i, t)

    def at_tile(s):
        return (sec, s)

    before, after = (t + n_tile - 1) % n_tile, (t + 1) % n_tile

    loads = [
        pltpu.make_async_copy(vec_ref, vec, load_sem.at[0]),
        pltpu.make_async_copy(classes_ref.at[0], cls, load_sem.at[1]),
    ]
    for load in loads:
        load.start()
    barrier = pltpu.get_barrier_semaphore()

    @pl.loop(1, line)
    def _(k):
        pl.semaphore_signal(barrier, inc=1, device_id=at_line((i + k) % line), device_id_type=MESH)

    for k in range(1, n_y):
        pl.semaphore_signal(barrier, inc=1, device_id=at_y((y + k) % n_y), device_id_type=MESH)
    for s in (before, after):
        pl.semaphore_signal(barrier, inc=1, device_id=at_tile(s), device_id_type=MESH)

    for r in range(2):
        ext[r, :, 0:8, :] = jnp.zeros((2, 8, width), F32)
        ext[r, :, rows + 8 :, :] = jnp.zeros((2, 8, width), F32)
    coef[:, 0:8, :] = jnp.zeros((4, 8, width), F32)
    coef[:, rows + 8 :, :] = jnp.zeros((4, 8, width), F32)

    pl.semaphore_wait(barrier, line - 1 + n_y - 1 + 2)

    def piece(field, j, base):
        top = pl.multiple_of(base + (j // per_row) * 8, 8)
        left = pl.multiple_of((j % per_row) * 128, 128)
        return field.at[:, pl.ds(top, 8), pl.ds(left, 128)]

    def send_in(field, r):
        pltpu.make_async_copy(piece(field, i, 0), fin.at[r, i], fin_recv_sem.at[r]).start()

        @pl.loop(1, line)
        def _(k):
            j = (i + k) % line
            pltpu.make_async_remote_copy(
                src_ref=piece(field, j, 0), dst_ref=fin.at[r, i],
                send_sem=fin_send_sem.at[r], recv_sem=fin_recv_sem.at[r],
                device_id=at_line(j), device_id_type=MESH,
            ).start()

    def wait_for(ref, sem):
        pltpu.make_async_copy(ref, ref, sem).wait()

    send_in(node_ref.at[0], 0)

    dest, slot = dest_ref[...], slot_ref[...]
    matches = dest.shape[1]
    hot = (iota((n_sec, matches), 0) == dest).astype(F32)
    earlier = (iota((matches, matches), 0) < iota((matches, matches), 1)).astype(BF16)
    hits = jnp.dot(hot.astype(BF16), earlier, preferred_element_type=F32)
    rank = jnp.sum(hot * hits, axis=0, keepdims=True).astype(jnp.int32)
    spot = (slot % per_row) * rows + slot // per_row
    base = 8 * n_y * (i % 4) + 8 * y + rank
    lane = iota((128, matches), 0)
    marks = jnp.where((lane == base) | (lane == base + CAP), (spot + 1).astype(F32), 0.0)
    sa_send[...] = lax.dot_general(
        hot.astype(BF16), marks.astype(BF16), (((1,), (1,)), ((), ())), preferred_element_type=F32
    ).reshape(n_y, line, 128)
    position = dest * 8 + rank
    position = jnp.concatenate([position, position + CAP], axis=1)
    loads[0].wait()
    vectors = vec[...]
    vectors = jnp.concatenate([vectors[:, :128], vectors[:, 128:]], axis=0)
    vectors = jnp.concatenate(split3(vectors), axis=1)
    for k in range(n_y):
        q = (y + k) % n_y
        place = (iota((line * 8, 2 * matches), 0) + q * (line * 8) == position).astype(F32).astype(BF16)
        packed = jnp.dot(place, vectors, preferred_element_type=F32)
        packed = (packed[:, :128] + packed[:, 128:256]) + packed[:, 256:]
        ma_send[q] = packed.reshape(line, 8, 128)
        if k == 0:
            pltpu.make_async_copy(ma_send.at[q], ma_recv.at[:, y], ma_recv_sem).start()
            pltpu.make_async_copy(sa_send.at[q], sa_recv.at[y], sa_recv_sem).start()
        else:
            pltpu.make_async_remote_copy(
                src_ref=ma_send.at[q], dst_ref=ma_recv.at[:, y], send_sem=ma_send_sem, recv_sem=ma_recv_sem,
                device_id=at_y(q), device_id_type=MESH,
            ).start()
            pltpu.make_async_remote_copy(
                src_ref=sa_send.at[q], dst_ref=sa_recv.at[y], send_sem=sa_send_sem, recv_sem=sa_recv_sem,
                device_id=at_y(q), device_id_type=MESH,
            ).start()

    z = jnp.broadcast_to(z_ref[...], (8, 128))
    p, tail, p_col, tail_col = inverse_parts(z, n_sec)
    full = p_col * (p * jnp.minimum(tail_col, tail))
    pt, pt_col = p * tail, p_col * tail_col
    block, p_own, pt_own = jnp.zeros((line, line), F32), jnp.zeros((1, line), F32), jnp.zeros((1, line), F32)
    p_own_col, pt_own_col = jnp.zeros((line, 1), F32), jnp.zeros((line, 1), F32)
    for q in range(n_y):
        here, cut = y == q, slice(q * line, (q + 1) * line)
        block = jnp.where(here, full[cut, cut], block)
        p_own, pt_own = jnp.where(here, p[:, cut], p_own), jnp.where(here, pt[:, cut], pt_own)
        p_own_col = jnp.where(here, p_col[cut], p_own_col)
        pt_own_col = jnp.where(here, pt_col[cut], pt_own_col)
    lhs[0:line, :] = block
    lhs[line : line + 8, :] = jnp.concatenate([p_own, pt_own, jnp.zeros((6, line), F32)], axis=0)
    cols[0] = jnp.broadcast_to(p_own_col, (line, 128))
    cols[1] = jnp.broadcast_to(pt_own_col, (line, 128))

    loads[1].wait()
    classes = cls[...]
    stiffness = jnp.zeros((rows, width), F32)
    for level in range(table_ref.shape[0]):
        stiffness = jnp.where(classes == level, table_ref[level], stiffness)
    coef[0, 8 : rows + 8, :] = RELAX * stiffness

    def forward_matches():
        wait_for(ma_recv, ma_recv_sem)
        wait_for(sa_recv, sa_recv_sem)
        marked = jnp.sum(sa_recv[...], axis=0)
        for j in range(line):
            sb_send[j] = marked[j : j + 1]
        pltpu.make_async_copy(sb_send.at[i], sb_recv.at[i], sb_recv_sem).start()
        pltpu.make_async_copy(ma_recv.at[i], mb_recv.at[i], mb_recv_sem).start()

        @pl.loop(1, line)
        def _(k):
            j = (i + k) % line
            pltpu.make_async_remote_copy(
                src_ref=sb_send.at[j], dst_ref=sb_recv.at[i], send_sem=sb_send_sem, recv_sem=sb_recv_sem,
                device_id=at_line(j), device_id_type=MESH,
            ).start()
            pltpu.make_async_remote_copy(
                src_ref=ma_recv.at[j], dst_ref=mb_recv.at[i], send_sem=mb_send_sem, recv_sem=mb_recv_sem,
                device_id=at_line(j), device_id_type=MESH,
            ).start()

    def place_matches():
        wait_for(sb_recv, sb_recv_sem)
        wait_for(mb_recv, mb_recv_sem)
        total = line * n_y * 8
        chunks = []
        for g in range(line // 4):
            chunks.append(jnp.sum(jnp.sum(sb_recv[4 * g : 4 * g + 4], axis=0), axis=0, keepdims=True)[:, : 32 * n_y])
        ids = jnp.concatenate(chunks, axis=1).astype(jnp.int32)
        comp = (iota((1, total), 1) // CAP) % 2
        rhs = mb_recv[...].reshape(total, 128)
        rhs = jnp.concatenate([*split3(rhs), jnp.ones((total, 128), BF16)], axis=1)
        spots = rows * per_row
        for c in range(2):
            target = jnp.where(comp == c, ids - 1, -1)
            chosen = (iota((spots, total), 0) == target).astype(F32).astype(BF16)
            sums = jnp.dot(chosen, rhs, preferred_element_type=F32)
            pulled = (sums[:, :128] + sums[:, 128:256]) + sums[:, 256:384]
            for b in range(per_row):
                cut = slice(b * rows, (b + 1) * rows)
                lanes = slice(b * 128, (b + 1) * 128)
                coef[2 + c, 8 : rows + 8, lanes] = RELAX * pulled[cut]
                if c == 0:
                    coef[1, 8 : rows + 8, lanes] = (
                        1.0 - 4.0 * coef[0, 8 : rows + 8, lanes] - RELAX * sums[cut, 384:]
                    )

    def solve(r):
        wait_for(fin.at[r], fin_recv_sem.at[r])
        f = jnp.concatenate([fin[r, :, c, s, :] for c in range(2) for s in range(8)], axis=1)
        got = jnp.dot(lhs[...], f, precision=lax.Precision.HIGHEST, preferred_element_type=F32)
        pq_send[r] = got[line : line + 2]
        pltpu.make_async_copy(pq_send.at[r], pq_recv.at[r, y], pq_recv_sem.at[r]).start()
        for k in range(1, n_y):
            pltpu.make_async_remote_copy(
                src_ref=pq_send.at[r], dst_ref=pq_recv.at[r, y], send_sem=pq_send_sem.at[r],
                recv_sem=pq_recv_sem.at[r], device_id=at_y((y + k) % n_y), device_id_type=MESH,
            ).start()
        if r == 0:
            forward_matches()
        wait_for(pq_recv.at[r], pq_recv_sem.at[r])
        below, above = jnp.zeros((1, 2048), F32), jnp.zeros((1, 2048), F32)
        for q in range(n_y):
            pair = pq_recv[r, q]
            below = below + jnp.where(q < y, pair[0:1], 0.0)
            above = above + jnp.where(q > y, pair[1:2], 0.0)
        for c in range(2):
            for s in range(8):
                cut = slice((c * 8 + s) * 128, (c * 8 + s + 1) * 128)
                xs[r, :, c, s, :] = got[0:line, cut] + cols[1] * below[:, cut] + cols[0] * above[:, cut]
        pltpu.make_async_copy(xs.at[r, i], piece(ext.at[r], i, 8), out_recv_sem.at[r]).start()

        @pl.loop(1, line)
        def _(k):
            j = (i + k) % line
            pltpu.make_async_remote_copy(
                src_ref=xs.at[r, j], dst_ref=piece(ext.at[r], i, 8),
                send_sem=out_send_sem.at[r], recv_sem=out_recv_sem.at[r],
                device_id=at_line(j), device_id_type=MESH,
            ).start()

    def halo(r):
        top = [ext[r, c, 8:10, :] for c in range(2)] + [coef[k, 8:9, :] for k in range(4)]
        last = rows + 8
        low = [ext[r, c, last - 2 : last, :] for c in range(2)] + [coef[k, last - 1 : last, :] for k in range(4)]
        halo_send[r, 0] = jnp.concatenate(top, axis=0)
        halo_send[r, 1] = jnp.concatenate(low, axis=0)
        for side, other in ((0, before), (1, after)):
            pltpu.make_async_remote_copy(
                src_ref=halo_send.at[r, side], dst_ref=halo_recv.at[r, side], send_sem=halo_send_sem.at[r],
                recv_sem=halo_recv_sem.at[r], device_id=at_tile(other), device_id_type=MESH,
            ).start()
        wait_for(halo_recv.at[r], halo_recv_sem.at[r])
        above = jnp.where(t > 0, halo_recv[r, 1], 0.0)
        below = jnp.where(t < n_tile - 1, halo_recv[r, 0], 0.0)
        for c in range(2):
            ext[r, c, 6:8, :] = above[2 * c : 2 * c + 2]
            ext[r, c, last : last + 2, :] = below[2 * c : 2 * c + 2]
        if r == 0:
            for k in range(4):
                coef[k, 7:8, :] = above[4 + k : 5 + k]
                coef[k, last : last + 1, :] = below[4 + k : 5 + k]

    def relax(r, store):
        height = rows + 16
        column = iota((height, width), 1)
        a, e = coef[0], coef[1]
        for c in range(2):
            v = ext[r, c]
            for _ in range(2):
                left = jnp.where(column == 0, 0.0, pltpu.roll(v, 1, 1))
                right = jnp.where(column == width - 1, 0.0, pltpu.roll(v, width - 1, 1))
                around = (pltpu.roll(v, 1, 0) + pltpu.roll(v, height - 1, 0)) + (left + right)
                v = e * v + (a * around + coef[2 + c])
            store(c, v[8 : rows + 8])

    def keep(c, v):
        fld[c] = v

    def finish(c, v):
        out_ref[0, c] = v

    for r in range(2):
        solve(r)
        if r == 0:
            place_matches()
        wait_for(ext.at[r, :, pl.ds(8, rows)], out_recv_sem.at[r])
        halo(r)
        if r == 0:
            relax(r, keep)
            send_in(fld, 1)
        else:
            relax(r, finish)

    for r in range(2):
        wait_for(fin.at[r, pl.ds(0, line - 1)], fin_send_sem.at[r])
        wait_for(xs.at[r, pl.ds(0, line - 1)], out_send_sem.at[r])
        wait_for(pq_recv.at[r, pl.ds(0, n_y - 1)], pq_send_sem.at[r])
        wait_for(halo_send.at[r], halo_send_sem.at[r])
    wait_for(ma_send.at[pl.ds(0, n_y - 1)], ma_send_sem)
    wait_for(sa_send.at[pl.ds(0, n_y - 1)], sa_send_sem)
    wait_for(mb_recv.at[pl.ds(0, line - 1)], mb_send_sem)
    wait_for(sb_recv.at[pl.ds(0, line - 1)], sb_send_sem)


def local(n_sec, n_tile, node_flow, classes, table, z_couple, match_dest, match_slot, match_vectors):
    _, comps, rows, width = node_flow.shape
    line = rows * width // 1024
    n_y = n_sec // line
    matches = match_vectors.shape[0]
    vmem, dma = pltpu.VMEM, pltpu.SemaphoreType.DMA
    z = jnp.pad(z_couple, (0, 128 - n_sec), constant_values=26.0).reshape(1, 128)
    return pl.pallas_call(
        functools.partial(kernel, (n_y, line, n_tile, rows, width)),
        out_shape=jax.ShapeDtypeStruct(node_flow.shape, F32),
        in_specs=[
            pl.BlockSpec(memory_space=pl.ANY),
            pl.BlockSpec(memory_space=pl.ANY),
            pl.BlockSpec(memory_space=pltpu.SMEM),
            pl.BlockSpec(memory_space=vmem),
            pl.BlockSpec(memory_space=vmem),
            pl.BlockSpec(memory_space=vmem),
            pl.BlockSpec(memory_space=pl.ANY),
        ],
        out_specs=pl.BlockSpec(memory_space=vmem),
        scratch_shapes=[
            vmem((2, line, 2, 8, 128), F32),
            vmem((2, line, 2, 8, 128), F32),
            vmem((2, 2, rows + 16, width), F32),
            vmem((2, rows, width), F32),
            vmem((2, 2, 2048), F32),
            vmem((2, n_y, 2, 2048), F32),
            vmem((line + 8, line), F32),
            vmem((2, line, 128), F32),
            vmem((n_y, line, 8, 128), F32),
            vmem((line, n_y, 8, 128), F32),
            vmem((line, n_y, 8, 128), F32),
            vmem((n_y, line, 128), F32),
            vmem((n_y, line, 128), F32),
            vmem((line, 1, 128), F32),
            vmem((line, 1, 128), F32),
            vmem((2, 2, 8, width), F32),
            vmem((2, 2, 8, width), F32),
            vmem((4, rows + 16, width), F32),
            vmem((rows, width), jnp.int32),
            vmem((matches, 256), F32),
            dma((2,)),
            *([dma((2,))] * 6),
            *([dma(())] * 8),
            *([dma((2,))] * 2),
        ],
        compiler_params=pltpu.CompilerParams(
            collective_id=0, has_side_effects=True, vmem_limit_bytes=48 * 1024 * 1024
        ),
        cost_estimate=pl.CostEstimate(flops=2 * 10**9, bytes_accessed=10**6, transcendentals=0),
        name="align",
    )(
        node_flow,
        classes,
        table,
        z,
        match_dest.reshape(1, matches),
        match_slot.reshape(1, matches),
        match_vectors,
    )


def solution(mesh):
    return jax.shard_map(
        functools.partial(local, mesh.shape["sec"], mesh.shape["tile"]),
        mesh=mesh,
        in_specs=(
            P("sec", None, "tile", None),
            P("sec", "tile", None),
            P(),
            P(),
            P(("sec", "tile"), None),
            P(("sec", "tile")),
            P(("sec", "tile"), None),
        ),
        out_specs=P("sec", None, "tile", None),
        check_vma=False,
    )
```

```python
import functools

import jax
import jax.numpy as jnp
from jax import lax
from jax.experimental import pallas as pl
from jax.experimental.pallas import tpu as pltpu
from jax.sharding import PartitionSpec as P

MESH = pl.DeviceIdType.MESH
RELAX = 0.05
CAP = 4
VMEM_LIMIT = 60 * 1024 * 1024
F32 = jnp.float32
BF16 = jnp.bfloat16


def iota(shape, dim):
    return lax.broadcasted_iota(jnp.int32, shape, dim)


def split3(v):
    hi = v.astype(BF16)
    rest = v - hi.astype(F32)
    mid = rest.astype(BF16)
    lo = (rest - mid.astype(F32)).astype(BF16)
    return hi, mid, lo


def inverse_parts(z, n):
    lanes = z.shape[1]
    lane = iota(z.shape, 1)
    w = 1.0 / z
    one = jnp.ones_like(z)
    m = (one, w, one, 1.0 + w)
    step = 1
    while step < n:
        first = lane < step
        b = [jnp.where(first, float(k in (0, 3)), pltpu.roll(v, step, 1)) for k, v in enumerate(m)]
        a = m
        m = (
            a[0] * b[0] + a[1] * b[2],
            a[0] * b[1] + a[1] * b[3],
            a[2] * b[0] + a[3] * b[2],
            a[2] * b[1] + a[3] * b[3],
        )
        step *= 2
    p_next = m[0] + m[1]
    p = jnp.where(lane == 0, 1.0, pltpu.roll(p_next, 1, 1))
    t = jnp.where(lane < n, 1.0 / (z * p * p_next), 0.0)
    p, t = p[:1], t[:1]
    r, c = iota((lanes, lanes), 0), iota((lanes, lanes), 1)
    p_col = jnp.sum(jnp.where(r == c, p, 0.0), axis=1, keepdims=True)
    tail_col = jnp.sum(jnp.where(c >= r, t, 0.0), axis=1, keepdims=True)
    return p_col, tail_col


def kernel(
    dims,
    node_ref, classes_ref, table_ref, z_ref, dest_ref, slot_ref, vec_ref, out_ref,
    fin, xs, ext, fld, pq_send, pq_recv, cols,
    ma_send, ma_recv, mb_recv, sa_send, sa_recv, sb_send, sb_recv,
    halo_send, halo_recv, coef, cls, vec, z_own, dest_own, slot_own, table,
    load_sem, fin_send_sem, fin_recv_sem, pq_send_sem, pq_recv_sem, out_send_sem, out_recv_sem,
    halo_send_sem, halo_recv_sem, ma_send_sem, ma_recv_sem, mb_send_sem, mb_recv_sem,
    sa_send_sem, sa_recv_sem, sb_send_sem, sb_recv_sem, store_sem,
):
    n_y, line, n_tile, rows, width = dims
    n_sec = n_y * line
    per_row = width // 128
    last = rows + 8
    sec, t = lax.axis_index("sec"), lax.axis_index("tile")
    y, i = sec // line, sec % line

    def at_line(j):
        return (y * line + j, t)

    def at_y(q):
        return (q * line + i, t)

    def at_tile(s):
        return (sec, s)

    def each_on_line(act):
        half = line // 2
        act((i + half) % line)

        @pl.loop(1, half)
        def _(k):
            act((i + half + k) % line)
            act((i + half - k) % line)

    def send(src, dst, send_sem, recv_sem, device):
        pltpu.make_async_remote_copy(
            src_ref=src, dst_ref=dst, send_sem=send_sem, recv_sem=recv_sem, device_id=device, device_id_type=MESH
        ).start()

    def keep(src, dst, sem):
        pltpu.make_async_copy(src, dst, sem).start()

    def wait_for(ref, sem):
        pltpu.make_async_copy(ref, ref, sem).wait()

    before, after = (t + n_tile - 1) % n_tile, (t + 1) % n_tile

    loads = [
        pltpu.make_async_copy(src, dst, load_sem.at[k])
        for k, (src, dst) in enumerate(
            (
                (dest_ref, dest_own),
                (slot_ref, slot_own),
                (vec_ref, vec),
                (z_ref, z_own),
                (table_ref, table),
                (classes_ref.at[0], cls),
            )
        )
    ]
    for load in loads:
        load.start()
    barrier = pltpu.get_barrier_semaphore()

    def greet(device):
        pl.semaphore_signal(barrier, inc=1, device_id=device, device_id_type=MESH)

    each_on_line(lambda j: greet(at_line(j)))
    for k in range(1, n_y):
        greet(at_y((y + k) % n_y))
    for s in (before, after):
        greet(at_tile(s))

    ext[:, :, 0:8, :] = jnp.zeros((2, 2, 8, width), F32)
    ext[:, :, last:, :] = jnp.zeros((2, 2, 8, width), F32)
    coef[:, 0:8, :] = jnp.zeros((4, 8, width), F32)
    coef[:, last:, :] = jnp.zeros((4, 8, width), F32)

    pl.semaphore_wait(barrier, line - 1 + n_y - 1 + 2)

    def piece(field, j, base):
        top = pl.multiple_of(base + (j // per_row) * 8, 8)
        left = pl.multiple_of((j % per_row) * 128, 128)
        return field.at[pl.ds(top, 8), pl.ds(left, 128)]

    def send_in(field, r, c):
        sems = fin_send_sem.at[r, c], fin_recv_sem.at[r, c]
        each_on_line(lambda j: send(piece(field, j, 0), fin.at[r, c, i], *sems, at_line(j)))
        keep(piece(field, i, 0), fin.at[r, c, i], sems[1])

    for c in range(2):
        send_in(node_ref.at[0, c], 0, c)

    loads[0].wait()
    loads[1].wait()
    dest, slot = dest_own[...], slot_own[...]
    matches = dest.shape[1]
    hot = (iota((n_sec, matches), 0) == dest).astype(F32)
    earlier = (iota((matches, matches), 0) < iota((matches, matches), 1)).astype(F32).astype(BF16)
    hits = jnp.dot(hot.astype(BF16), earlier, preferred_element_type=F32)
    rank = jnp.sum(hot * hits, axis=0, keepdims=True).astype(jnp.int32)
    spot = (slot % per_row) * rows + slot // per_row
    group = 128 // (CAP * n_y)
    base = CAP * n_y * (i % group) + CAP * y + rank
    marks = jnp.where(iota((128, matches), 0) == base, (spot + 1).astype(F32), 0.0)
    sa_send[...] = lax.dot_general(
        hot.astype(BF16), marks.astype(BF16), (((1,), (1,)), ((), ())), preferred_element_type=F32
    ).reshape(n_y, line, 128)
    position = dest * CAP + rank
    loads[2].wait()
    vectors = jnp.concatenate(split3(vec[...]), axis=1)
    for k in range(n_y):
        q = (y + k) % n_y
        place = (iota((line * CAP, matches), 0) + q * (line * CAP) == position).astype(F32).astype(BF16)
        packed = jnp.dot(place, vectors, preferred_element_type=F32)
        packed = (packed[:, :256] + packed[:, 256:512]) + packed[:, 512:]
        for c in range(2):
            ma_send[c, q] = packed[:, c * 128 : c * 128 + 128].reshape(line, CAP, 128)
            if k == 0:
                keep(ma_send.at[c, q], ma_recv.at[c, y], ma_recv_sem.at[c])
            else:
                send(ma_send.at[c, q], ma_recv.at[c, y], ma_send_sem.at[c], ma_recv_sem.at[c], at_y(q))
        if k == 0:
            keep(sa_send.at[q], sa_recv.at[y], sa_recv_sem)
        else:
            send(sa_send.at[q], sa_recv.at[y], sa_send_sem, sa_recv_sem, at_y(q))

    loads[3].wait()
    p_col, tail_col = inverse_parts(jnp.broadcast_to(z_own[...], (8, 128)), n_sec)
    pt_col = p_col * tail_col
    p_own, pt_own = p_col[:line], pt_col[:line]
    for q in range(1, n_y):
        cut = slice(q * line, (q + 1) * line)
        p_own, pt_own = jnp.where(y == q, p_col[cut], p_own), jnp.where(y == q, pt_col[cut], pt_own)
    cols[0] = jnp.broadcast_to(p_own, (line, 128))
    cols[1] = jnp.broadcast_to(pt_own, (line, 128))

    loads[4].wait()
    loads[5].wait()
    classes = cls[...]
    stiffness = jnp.zeros((rows, width), F32)
    for level in range(table.shape[0]):
        stiffness = jnp.where(classes == level, table[level], stiffness)
    coef[0, 8:last, :] = RELAX * stiffness

    def forward_slots():
        wait_for(sa_recv, sa_recv_sem)
        marked = jnp.sum(sa_recv[...], axis=0)
        for j in range(line):
            sb_send[j] = marked[j : j + 1]
        each_on_line(lambda j: send(sb_send.at[j], sb_recv.at[i], sb_send_sem, sb_recv_sem, at_line(j)))
        keep(sb_send.at[i], sb_recv.at[i], sb_recv_sem)

    def forward_matches(c):
        wait_for(ma_recv.at[c], ma_recv_sem.at[c])
        each_on_line(
            lambda j: send(ma_recv.at[c, :, j], mb_recv.at[c, i], mb_send_sem.at[c], mb_recv_sem.at[c], at_line(j))
        )
        keep(ma_recv.at[c, :, i], mb_recv.at[c, i], mb_recv_sem.at[c])

    spots, total = rows * per_row, line * n_y * CAP

    def choose():
        wait_for(sb_recv, sb_recv_sem)
        used = min(group, line)
        chunks = []
        for g in range(line // used):
            part = jnp.sum(jnp.sum(sb_recv[used * g : used * (g + 1)], axis=0), axis=0, keepdims=True)
            chunks.append(part[:, : used * n_y * CAP])
        ids = jnp.concatenate(chunks, axis=1).astype(jnp.int32) - 1
        chosen = (iota((spots, total), 0) == ids).astype(F32)
        counts = jnp.broadcast_to(jnp.sum(chosen, axis=1, keepdims=True), (spots, 128))
        for b in range(per_row):
            lanes = slice(b * 128, (b + 1) * 128)
            coef[1, 8:last, lanes] = (
                1.0 - 4.0 * coef[0, 8:last, lanes] - RELAX * counts[b * rows : (b + 1) * rows]
            )
        return chosen.astype(BF16)

    def place_matches(c, chosen):
        wait_for(mb_recv.at[c], mb_recv_sem.at[c])
        rhs = jnp.concatenate(split3(mb_recv[c].reshape(total, 128)), axis=1)
        sums = jnp.dot(chosen, rhs, preferred_element_type=F32)
        pulled = RELAX * ((sums[:, :128] + sums[:, 128:256]) + sums[:, 256:])
        for b in range(per_row):
            coef[2 + c, 8:last, b * 128 : (b + 1) * 128] = pulled[b * rows : (b + 1) * rows]

    def totals(r, c):
        wait_for(fin.at[r, c], fin_recv_sem.at[r, c])
        low, high = jnp.zeros((8, 128), F32), jnp.zeros((8, 128), F32)
        for j in range(line):
            f = fin[r, c, j]
            low, high = low + cols[0, j : j + 1] * f, high + cols[1, j : j + 1] * f
        pq_send[r, c, 0], pq_send[r, c, 1] = low, high
        sems = pq_send_sem.at[r, c], pq_recv_sem.at[r, c]
        for k in range(1, n_y):
            send(pq_send.at[r, c], pq_recv.at[r, c, y], *sems, at_y((y + k) % n_y))
        keep(pq_send.at[r, c], pq_recv.at[r, c, y], sems[1])

    def solve(r, c):
        wait_for(pq_recv.at[r, c], pq_recv_sem.at[r, c])
        low, high = jnp.zeros((8, 128), F32), jnp.zeros((8, 128), F32)
        for q in range(n_y):
            low = low + jnp.where(q < y, pq_recv[r, c, q, 0], 0.0)
            high = high + jnp.where(q > y, pq_recv[r, c, q, 1], 0.0)
        for j in range(line):
            low = low + cols[0, j : j + 1] * fin[r, c, j]
            xs[r, c, j] = cols[1, j : j + 1] * low
        for j in reversed(range(line)):
            xs[r, c, j] = xs[r, c, j] + cols[0, j : j + 1] * high
            high = high + cols[1, j : j + 1] * fin[r, c, j]
        spot_there = piece(ext.at[r, c], i, 8)
        sems = out_send_sem.at[r, c], out_recv_sem.at[r, c]
        each_on_line(lambda j: send(xs.at[r, c, j], spot_there, *sems, at_line(j)))
        keep(xs.at[r, c, i], spot_there, sems[1])

    def send_halo(r, c):
        wait_for(ext.at[r, c, pl.ds(8, rows)], out_recv_sem.at[r, c])
        which = ([2 + c, 0, 1] if c == 0 else [2 + c]) if r == 0 else []
        for side, other, near, edge in ((0, before, 8, 8), (1, after, last - 2, last - 1)):
            halo_send[r, c, side, 0:2, :] = ext[r, c, near : near + 2, :]
            for k, w in enumerate(which):
                halo_send[r, c, side, 2 + k : 3 + k, :] = coef[w, edge : edge + 1, :]
            send(
                halo_send.at[r, c, side], halo_recv.at[r, c, side],
                halo_send_sem.at[r, c], halo_recv_sem.at[r, c], at_tile(other),
            )

    def relax(r, c):
        wait_for(halo_recv.at[r, c], halo_recv_sem.at[r, c])
        above = jnp.where(t > 0, halo_recv[r, c, 1], 0.0)
        below = jnp.where(t < n_tile - 1, halo_recv[r, c, 0], 0.0)
        ext[r, c, 6:8, :] = above[0:2]
        ext[r, c, last : last + 2, :] = below[0:2]
        which = ([2 + c, 0, 1] if c == 0 else [2 + c]) if r == 0 else []
        for k, w in enumerate(which):
            coef[w, 7:8, :] = above[2 + k : 3 + k]
            coef[w, last : last + 1, :] = below[2 + k : 3 + k]
        height = rows + 16
        column = iota((height, width), 1)
        v = ext[r, c]
        for _ in range(2):
            left = jnp.where(column == 0, 0.0, pltpu.roll(v, 1, 1))
            right = jnp.where(column == width - 1, 0.0, pltpu.roll(v, width - 1, 1))
            around = (pltpu.roll(v, 1, 0) + pltpu.roll(v, height - 1, 0)) + (left + right)
            v = coef[1] * v + (coef[0] * around + coef[2 + c])
        fld[r, c] = v[8:last]

    forward_slots()
    forward_matches(0)
    totals(0, 0)
    totals(0, 1)
    solve(0, 0)
    forward_matches(1)
    solve(0, 1)
    chosen = choose()
    place_matches(0, chosen)
    send_halo(0, 0)
    relax(0, 0)
    send_in(fld.at[0, 0], 1, 0)
    place_matches(1, chosen)
    send_halo(0, 1)
    totals(1, 0)
    relax(0, 1)
    send_in(fld.at[0, 1], 1, 1)
    solve(1, 0)
    totals(1, 1)
    solve(1, 1)
    for c in range(2):
        send_halo(1, c)
        relax(1, c)
        keep(fld.at[1, c], out_ref.at[0, c], store_sem.at[c])

    for c in range(2):
        for r in range(2):
            wait_for(fin.at[r, c, pl.ds(0, line - 1)], fin_send_sem.at[r, c])
            wait_for(xs.at[r, c, pl.ds(0, line - 1)], out_send_sem.at[r, c])
            wait_for(pq_recv.at[r, c, pl.ds(0, n_y - 1)], pq_send_sem.at[r, c])
            wait_for(halo_send.at[r, c], halo_send_sem.at[r, c])
        wait_for(ma_send.at[c, pl.ds(0, n_y - 1)], ma_send_sem.at[c])
        wait_for(mb_recv.at[c, pl.ds(0, line - 1)], mb_send_sem.at[c])
    wait_for(sa_send.at[pl.ds(0, n_y - 1)], sa_send_sem)
    wait_for(sb_recv.at[pl.ds(0, line - 1)], sb_send_sem)
    for c in range(2):
        pltpu.make_async_copy(fld.at[1, c], out_ref.at[0, c], store_sem.at[c]).wait()


def local(n_sec, n_tile, node_flow, classes, table, z_couple, match_dest, match_slot, match_vectors):
    _, comps, rows, width = node_flow.shape
    line = rows * width // 1024
    n_y = n_sec // line
    matches = match_vectors.shape[0]
    vmem, dma = pltpu.VMEM, pltpu.SemaphoreType.DMA
    z = jnp.pad(z_couple, (0, 128 - n_sec), constant_values=26.0).reshape(1, 128)
    return pl.pallas_call(
        functools.partial(kernel, (n_y, line, n_tile, rows, width)),
        out_shape=jax.ShapeDtypeStruct(node_flow.shape, F32),
        in_specs=[pl.BlockSpec(memory_space=pl.ANY)] * 7,
        out_specs=pl.BlockSpec(memory_space=pl.ANY),
        scratch_shapes=[
            vmem((2, 2, line, 8, 128), F32),
            vmem((2, 2, line, 8, 128), F32),
            vmem((2, 2, rows + 16, width), F32),
            vmem((2, 2, rows, width), F32),
            vmem((2, 2, 2, 8, 128), F32),
            vmem((2, 2, n_y, 2, 8, 128), F32),
            vmem((2, line, 128), F32),
            vmem((2, n_y, line, CAP, 128), F32),
            vmem((2, n_y, line, CAP, 128), F32),
            vmem((2, line, n_y, CAP, 128), F32),
            vmem((n_y, line, 128), F32),
            vmem((n_y, line, 128), F32),
            vmem((line, 1, 128), F32),
            vmem((line, 1, 128), F32),
            vmem((2, 2, 2, 8, width), F32),
            vmem((2, 2, 2, 8, width), F32),
            vmem((4, rows + 16, width), F32),
            vmem((rows, width), jnp.int32),
            vmem((matches, 256), F32),
            vmem((1, 128), F32),
            vmem((1, matches), jnp.int32),
            vmem((1, matches), jnp.int32),
            pltpu.SMEM((table.shape[0],), F32),
            dma((6,)),
            *([dma((2, 2))] * 8),
            *([dma((2,))] * 4),
            *([dma(())] * 4),
            dma((2,)),
        ],
        compiler_params=pltpu.CompilerParams(
            collective_id=0, has_side_effects=True, vmem_limit_bytes=VMEM_LIMIT
        ),
        cost_estimate=pl.CostEstimate(flops=10**9, bytes_accessed=10**6, transcendentals=0),
        name="align",
    )(
        node_flow,
        classes,
        table,
        z,
        match_dest.reshape(1, matches),
        match_slot.reshape(1, matches),
        match_vectors,
    )


def solution(mesh):
    return jax.shard_map(
        functools.partial(local, mesh.shape["sec"], mesh.shape["tile"]),
        mesh=mesh,
        in_specs=(
            P("sec", None, "tile", None),
            P("sec", "tile", None),
            P(),
            P(),
            P(("sec", "tile"), None),
            P(("sec", "tile")),
            P(("sec", "tile"), None),
        ),
        out_specs=P("sec", None, "tile", None),
        check_vma=False,
    )
```

```python
import functools

import jax
import jax.numpy as jnp
from jax import lax
from jax.experimental import pallas as pl
from jax.experimental.pallas import tpu as pltpu
from jax.sharding import PartitionSpec as P

MESH = pl.DeviceIdType.MESH
RELAX = 0.05
CAP = 4
VMEM_LIMIT = 60 * 1024 * 1024
F32 = jnp.float32
BF16 = jnp.bfloat16


def iota(shape, dim):
    return lax.broadcasted_iota(jnp.int32, shape, dim)


def split3(v):
    hi = v.astype(BF16)
    rest = v - hi.astype(F32)
    mid = rest.astype(BF16)
    lo = (rest - mid.astype(F32)).astype(BF16)
    return hi, mid, lo


def inverse_parts(z, n):
    lanes = z.shape[1]
    lane = iota(z.shape, 1)
    w = 1.0 / z
    one = jnp.ones_like(z)
    m = (one, w, one, 1.0 + w)
    step = 1
    while step < n:
        first = lane < step
        b = [jnp.where(first, float(k in (0, 3)), pltpu.roll(v, step, 1)) for k, v in enumerate(m)]
        a = m
        m = (
            a[0] * b[0] + a[1] * b[2],
            a[0] * b[1] + a[1] * b[3],
            a[2] * b[0] + a[3] * b[2],
            a[2] * b[1] + a[3] * b[3],
        )
        step *= 2
    p_next = m[0] + m[1]
    p = jnp.where(lane == 0, 1.0, pltpu.roll(p_next, 1, 1))
    t = jnp.where(lane < n, 1.0 / (z * p * p_next), 0.0)
    p, t = p[:1], t[:1]
    r, c = iota((lanes, lanes), 0), iota((lanes, lanes), 1)
    p_col = jnp.sum(jnp.where(r == c, p, 0.0), axis=1, keepdims=True)
    tail_col = jnp.sum(jnp.where(c >= r, t, 0.0), axis=1, keepdims=True)
    return p_col, tail_col


def kernel(
    dims,
    node_ref, classes_ref, table_ref, z_ref, dest_ref, slot_ref, vec_ref, out_ref,
    fin, xs, ext, fld, pq_send, pq_recv, cols,
    ma_send, ma_recv, mb_recv, sa_send, sa_recv, sb_send, sb_recv,
    edge_send, edge_recv, side_send, side_recv, coef, cls, vec, z_own, dest_own, slot_own, table,
    load_sem, fin_send_sem, fin_recv_sem, pq_send_sem, pq_recv_sem, out_send_sem, out_recv_sem,
    edge_send_sem, edge_recv_sem, side_send_sem, side_recv_sem, ma_send_sem, ma_recv_sem, mb_send_sem, mb_recv_sem,
    sa_send_sem, sa_recv_sem, sb_send_sem, sb_recv_sem, store_sem,
):
    n_y, line, n_tile, rows, width = dims
    n_sec = n_y * line
    per_row = width // 128
    last = rows + 8
    tops = rows // 8
    sec, t = lax.axis_index("sec"), lax.axis_index("tile")
    y, i = sec // line, sec % line

    def at_line(j):
        return (y * line + j, t)

    def at_y(q):
        return (q * line + i, t)

    def at_tile(s):
        return (sec, s)

    def each_on_line(act):
        half = line // 2
        act((i + half) % line)

        @pl.loop(1, half)
        def _(k):
            act((i + half + k) % line)
            act((i + half - k) % line)

    def send(src, dst, send_sem, recv_sem, device):
        pltpu.make_async_remote_copy(
            src_ref=src, dst_ref=dst, send_sem=send_sem, recv_sem=recv_sem, device_id=device, device_id_type=MESH
        ).start()

    def keep(src, dst, sem):
        pltpu.make_async_copy(src, dst, sem).start()

    def wait_for(ref, sem):
        pltpu.make_async_copy(ref, ref, sem).wait()

    before, after = (t + n_tile - 1) % n_tile, (t + 1) % n_tile

    loads = [
        pltpu.make_async_copy(src, dst, load_sem.at[k])
        for k, (src, dst) in enumerate(
            (
                (dest_ref, dest_own),
                (slot_ref, slot_own),
                (vec_ref, vec),
                (z_ref, z_own),
                (table_ref, table),
                (classes_ref.at[0], cls),
            )
        )
    ]
    for load in loads:
        load.start()
    barrier = pltpu.get_barrier_semaphore()

    def greet(device):
        pl.semaphore_signal(barrier, inc=1, device_id=device, device_id_type=MESH)

    each_on_line(lambda j: greet(at_line(j)))
    for k in range(1, n_y):
        greet(at_y((y + k) % n_y))
    for s in (before, after):
        greet(at_tile(s))
    for k in range(per_row):
        greet((y * line + k * tops, after))
        greet((y * line + k * tops + 1 % tops, before))

    ext[:, :, 0:8, :] = jnp.zeros((2, 2, 8, width), F32)
    ext[:, :, last:, :] = jnp.zeros((2, 2, 8, width), F32)
    coef[:, 0:8, :] = jnp.zeros((4, 8, width), F32)
    coef[:, last:, :] = jnp.zeros((4, 8, width), F32)

    on_top = i % tops == 0
    on_bottom = i % tops == 1 % tops
    edges = on_top.astype(jnp.int32) + on_bottom.astype(jnp.int32)
    pl.semaphore_wait(barrier, line - 1 + n_y - 1 + 2 + line * edges)

    def piece(field, j, base):
        top = pl.multiple_of(base + (tops - j % tops) % tops * 8, 8)
        left = pl.multiple_of(j // tops * 128, 128)
        return field.at[pl.ds(top, 8), pl.ds(left, 128)]

    def send_in(field, r, c):
        sems = fin_send_sem.at[r, c], fin_recv_sem.at[r, c]
        each_on_line(lambda j: send(piece(field, j, 0), fin.at[r, c, i], *sems, at_line(j)))
        keep(piece(field, i, 0), fin.at[r, c, i], sems[1])

    for c in range(2):
        send_in(node_ref.at[0, c], 0, c)

    loads[0].wait()
    loads[1].wait()
    dest, slot = dest_own[...], slot_own[...]
    matches = dest.shape[1]
    hot = (iota((n_sec, matches), 0) == dest).astype(F32)
    earlier = (iota((matches, matches), 0) < iota((matches, matches), 1)).astype(F32).astype(BF16)
    hits = jnp.dot(hot.astype(BF16), earlier, preferred_element_type=F32)
    rank = jnp.sum(hot * hits, axis=0, keepdims=True).astype(jnp.int32)
    spot = (slot % per_row) * rows + slot // per_row
    group = 128 // (CAP * n_y)
    base = CAP * n_y * (i % group) + CAP * y + rank
    marks = jnp.where(iota((128, matches), 0) == base, (spot + 1).astype(F32), 0.0)
    sa_send[...] = lax.dot_general(
        hot.astype(BF16), marks.astype(BF16), (((1,), (1,)), ((), ())), preferred_element_type=F32
    ).reshape(n_y, line, 128)
    position = dest * CAP + rank
    loads[2].wait()
    vectors = jnp.concatenate(split3(vec[...]), axis=1)
    for k in range(n_y):
        q = (y + k) % n_y
        place = (iota((line * CAP, matches), 0) + q * (line * CAP) == position).astype(F32).astype(BF16)
        packed = jnp.dot(place, vectors, preferred_element_type=F32)
        packed = (packed[:, :256] + packed[:, 256:512]) + packed[:, 512:]
        for c in range(2):
            ma_send[c, q] = packed[:, c * 128 : c * 128 + 128].reshape(line, CAP, 128)
            if k == 0:
                keep(ma_send.at[c, q], ma_recv.at[c, y], ma_recv_sem.at[c])
            else:
                send(ma_send.at[c, q], ma_recv.at[c, y], ma_send_sem.at[c], ma_recv_sem.at[c], at_y(q))
        if k == 0:
            keep(sa_send.at[q], sa_recv.at[y], sa_recv_sem)
        else:
            send(sa_send.at[q], sa_recv.at[y], sa_send_sem, sa_recv_sem, at_y(q))

    loads[3].wait()
    p_col, tail_col = inverse_parts(jnp.broadcast_to(z_own[...], (8, 128)), n_sec)
    pt_col = p_col * tail_col
    p_own, pt_own = p_col[:line], pt_col[:line]
    for q in range(1, n_y):
        cut = slice(q * line, (q + 1) * line)
        p_own, pt_own = jnp.where(y == q, p_col[cut], p_own), jnp.where(y == q, pt_col[cut], pt_own)
    cols[0] = jnp.broadcast_to(p_own, (line, 128))
    cols[1] = jnp.broadcast_to(pt_own, (line, 128))

    loads[4].wait()
    loads[5].wait()
    classes = cls[...]
    stiffness = jnp.zeros((rows, width), F32)
    for level in range(table.shape[0]):
        stiffness = jnp.where(classes == level, table[level], stiffness)
    coef[0, 8:last, :] = RELAX * stiffness

    def forward_slots():
        wait_for(sa_recv, sa_recv_sem)
        marked = jnp.sum(sa_recv[...], axis=0)
        for j in range(line):
            sb_send[j] = marked[j : j + 1]
        each_on_line(lambda j: send(sb_send.at[j], sb_recv.at[i], sb_send_sem, sb_recv_sem, at_line(j)))
        keep(sb_send.at[i], sb_recv.at[i], sb_recv_sem)

    def forward_matches(c):
        wait_for(ma_recv.at[c], ma_recv_sem.at[c])
        each_on_line(
            lambda j: send(ma_recv.at[c, :, j], mb_recv.at[c, i], mb_send_sem.at[c], mb_recv_sem.at[c], at_line(j))
        )
        keep(ma_recv.at[c, :, i], mb_recv.at[c, i], mb_recv_sem.at[c])

    spots, total = rows * per_row, line * n_y * CAP

    def choose():
        wait_for(sb_recv, sb_recv_sem)
        used = min(group, line)
        chunks = []
        for g in range(line // used):
            part = jnp.sum(jnp.sum(sb_recv[used * g : used * (g + 1)], axis=0), axis=0, keepdims=True)
            chunks.append(part[:, : used * n_y * CAP])
        ids = jnp.concatenate(chunks, axis=1).astype(jnp.int32) - 1
        chosen = (iota((spots, total), 0) == ids).astype(F32)
        counts = jnp.broadcast_to(jnp.sum(chosen, axis=1, keepdims=True), (spots, 128))
        for b in range(per_row):
            lanes = slice(b * 128, (b + 1) * 128)
            coef[1, 8:last, lanes] = (
                1.0 - 4.0 * coef[0, 8:last, lanes] - RELAX * counts[b * rows : (b + 1) * rows]
            )
        return chosen.astype(BF16)

    def place_matches(c, chosen):
        wait_for(mb_recv.at[c], mb_recv_sem.at[c])
        rhs = jnp.concatenate(split3(mb_recv[c].reshape(total, 128)), axis=1)
        sums = jnp.dot(chosen, rhs, preferred_element_type=F32)
        pulled = RELAX * ((sums[:, :128] + sums[:, 128:256]) + sums[:, 256:])
        for b in range(per_row):
            coef[2 + c, 8:last, b * 128 : (b + 1) * 128] = pulled[b * rows : (b + 1) * rows]

    def totals(r, c):
        wait_for(fin.at[r, c], fin_recv_sem.at[r, c])
        low, high = jnp.zeros((8, 128), F32), jnp.zeros((8, 128), F32)
        for j in range(line):
            f = fin[r, c, j]
            low, high = low + cols[0, j : j + 1] * f, high + cols[1, j : j + 1] * f
        pq_send[r, c, 0], pq_send[r, c, 1] = low, high
        sems = pq_send_sem.at[r, c], pq_recv_sem.at[r, c]
        for k in range(1, n_y):
            send(pq_send.at[r, c], pq_recv.at[r, c, y], *sems, at_y((y + k) % n_y))
        keep(pq_send.at[r, c], pq_recv.at[r, c, y], sems[1])

    def solve(r, c):
        wait_for(pq_recv.at[r, c], pq_recv_sem.at[r, c])
        low, high = jnp.zeros((8, 128), F32), jnp.zeros((8, 128), F32)
        for q in range(n_y):
            low = low + jnp.where(q < y, pq_recv[r, c, q, 0], 0.0)
            high = high + jnp.where(q > y, pq_recv[r, c, q, 1], 0.0)
        for j in range(line):
            low = low + cols[0, j : j + 1] * fin[r, c, j]
            xs[r, c, j] = cols[1, j : j + 1] * low
        for j in reversed(range(line)):
            xs[r, c, j] = xs[r, c, j] + cols[0, j : j + 1] * high
            high = high + cols[1, j : j + 1] * fin[r, c, j]
        spot_there = piece(ext.at[r, c], i, 8)
        sems = out_send_sem.at[r, c], out_recv_sem.at[r, c]
        for side, here in ((0, on_top), (1, on_bottom)):

            @pl.when(here)
            def _():
                for j in range(line):
                    edge_send[r, c, side, j] = xs[r, c, j, 6 * side : 6 * side + 2]

        def over(j, side, beyond):
            send(
                edge_send.at[r, c, side, j], edge_recv.at[r, c, side, i // tops],
                edge_send_sem.at[r, c, side], edge_recv_sem.at[r, c, side], (y * line + j, beyond),
            )

        def both(j):
            for side, here, beyond in ((0, on_top, before), (1, on_bottom, after)):

                @pl.when(here)
                def _():
                    over(j, side, beyond)

            send(xs.at[r, c, j], spot_there, *sems, at_line(j))

        each_on_line(both)
        for side, here, beyond in ((0, on_top, before), (1, on_bottom, after)):

            @pl.when(here)
            def _():
                over(i, side, beyond)

        keep(xs.at[r, c, i], spot_there, sems[1])

    def send_sides(c):
        which = [2, 0, 1] if c == 0 else [3]
        for side, other, edge in ((0, before, 8), (1, after, last - 1)):
            for k, w in enumerate(which):
                side_send[c, side, k : k + 1, :] = coef[w, edge : edge + 1, :]
            send(
                side_send.at[c, side], side_recv.at[c, side], side_send_sem.at[c], side_recv_sem.at[c], at_tile(other)
            )

    def relax(r, c):
        if r == 0:
            wait_for(side_recv.at[c], side_recv_sem.at[c])
            above = jnp.where(t > 0, side_recv[c, 1], 0.0)
            below = jnp.where(t < n_tile - 1, side_recv[c, 0], 0.0)
            for k, w in enumerate([2, 0, 1] if c == 0 else [3]):
                coef[w, 7:8, :] = above[k : k + 1]
                coef[w, last : last + 1, :] = below[k : k + 1]
        for side in range(2):
            wait_for(edge_recv.at[r, c, side], edge_recv_sem.at[r, c, side])
        for b in range(per_row):
            lanes = slice(b * 128, (b + 1) * 128)
            ext[r, c, 6:8, lanes] = jnp.where(t > 0, edge_recv[r, c, 1, b], 0.0)
            ext[r, c, last : last + 2, lanes] = jnp.where(t < n_tile - 1, edge_recv[r, c, 0, b], 0.0)
        wait_for(ext.at[r, c, pl.ds(8, rows)], out_recv_sem.at[r, c])
        height = rows + 16
        column = iota((height, width), 1)
        v = ext[r, c]
        for _ in range(2):
            left = jnp.where(column == 0, 0.0, pltpu.roll(v, 1, 1))
            right = jnp.where(column == width - 1, 0.0, pltpu.roll(v, width - 1, 1))
            around = (pltpu.roll(v, 1, 0) + pltpu.roll(v, height - 1, 0)) + (left + right)
            v = coef[1] * v + (coef[0] * around + coef[2 + c])
        fld[r, c] = v[8:last]

    forward_matches(0)
    forward_slots()
    totals(0, 0)
    totals(0, 1)
    solve(0, 0)
    forward_matches(1)
    solve(0, 1)
    chosen = choose()
    place_matches(0, chosen)
    send_sides(0)
    relax(0, 0)
    send_in(fld.at[0, 0], 1, 0)
    place_matches(1, chosen)
    send_sides(1)
    relax(0, 1)
    send_in(fld.at[0, 1], 1, 1)
    totals(1, 0)
    solve(1, 0)
    totals(1, 1)
    solve(1, 1)
    for c in range(2):
        relax(1, c)
        keep(fld.at[1, c], out_ref.at[0, c], store_sem.at[c])

    for c in range(2):
        for r in range(2):
            wait_for(fin.at[r, c, pl.ds(0, line - 1)], fin_send_sem.at[r, c])
            wait_for(xs.at[r, c, pl.ds(0, line - 1)], out_send_sem.at[r, c])
            wait_for(pq_recv.at[r, c, pl.ds(0, n_y - 1)], pq_send_sem.at[r, c])
            for side, here in ((0, on_top), (1, on_bottom)):

                @pl.when(here)
                def _():
                    wait_for(edge_send.at[r, c, side], edge_send_sem.at[r, c, side])

        wait_for(ma_send.at[c, pl.ds(0, n_y - 1)], ma_send_sem.at[c])
        wait_for(mb_recv.at[c, pl.ds(0, line - 1)], mb_send_sem.at[c])
        wait_for(side_send.at[c], side_send_sem.at[c])
    wait_for(sa_send.at[pl.ds(0, n_y - 1)], sa_send_sem)
    wait_for(sb_recv.at[pl.ds(0, line - 1)], sb_send_sem)
    for c in range(2):
        pltpu.make_async_copy(fld.at[1, c], out_ref.at[0, c], store_sem.at[c]).wait()


def local(n_sec, n_tile, node_flow, classes, table, z_couple, match_dest, match_slot, match_vectors):
    _, comps, rows, width = node_flow.shape
    line = rows * width // 1024
    n_y = n_sec // line
    matches = match_vectors.shape[0]
    vmem, dma = pltpu.VMEM, pltpu.SemaphoreType.DMA
    z = jnp.pad(z_couple, (0, 128 - n_sec), constant_values=26.0).reshape(1, 128)
    return pl.pallas_call(
        functools.partial(kernel, (n_y, line, n_tile, rows, width)),
        out_shape=jax.ShapeDtypeStruct(node_flow.shape, F32),
        in_specs=[pl.BlockSpec(memory_space=pl.ANY)] * 7,
        out_specs=pl.BlockSpec(memory_space=pl.ANY),
        scratch_shapes=[
            vmem((2, 2, line, 8, 128), F32),
            vmem((2, 2, line, 8, 128), F32),
            vmem((2, 2, rows + 16, width), F32),
            vmem((2, 2, rows, width), F32),
            vmem((2, 2, 2, 8, 128), F32),
            vmem((2, 2, n_y, 2, 8, 128), F32),
            vmem((2, line, 128), F32),
            vmem((2, n_y, line, CAP, 128), F32),
            vmem((2, n_y, line, CAP, 128), F32),
            vmem((2, line, n_y, CAP, 128), F32),
            vmem((n_y, line, 128), F32),
            vmem((n_y, line, 128), F32),
            vmem((line, 1, 128), F32),
            vmem((line, 1, 128), F32),
            vmem((2, 2, 2, line, 2, 128), F32),
            vmem((2, 2, 2, width // 128, 2, 128), F32),
            vmem((2, 2, 8, width), F32),
            vmem((2, 2, 8, width), F32),
            vmem((4, rows + 16, width), F32),
            vmem((rows, width), jnp.int32),
            vmem((matches, 256), F32),
            vmem((1, 128), F32),
            vmem((1, matches), jnp.int32),
            vmem((1, matches), jnp.int32),
            pltpu.SMEM((table.shape[0],), F32),
            dma((6,)),
            *([dma((2, 2))] * 6),
            *([dma((2, 2, 2))] * 2),
            *([dma((2,))] * 6),
            *([dma(())] * 4),
            dma((2,)),
        ],
        compiler_params=pltpu.CompilerParams(
            collective_id=0, has_side_effects=True, vmem_limit_bytes=VMEM_LIMIT
        ),
        cost_estimate=pl.CostEstimate(flops=10**9, bytes_accessed=10**6, transcendentals=0),
        name="align",
    )(
        node_flow,
        classes,
        table,
        z,
        match_dest.reshape(1, matches),
        match_slot.reshape(1, matches),
        match_vectors,
    )


def solution(mesh):
    return jax.shard_map(
        functools.partial(local, mesh.shape["sec"], mesh.shape["tile"]),
        mesh=mesh,
        in_specs=(
            P("sec", None, "tile", None),
            P("sec", "tile", None),
            P(),
            P(),
            P(("sec", "tile"), None),
            P(("sec", "tile")),
            P(("sec", "tile"), None),
        ),
        out_specs=P("sec", None, "tile", None),
        check_vma=False,
    )
```

```python
import functools

import jax
import jax.numpy as jnp
from jax import lax
from jax.experimental import pallas as pl
from jax.experimental.pallas import tpu as pltpu
from jax.sharding import PartitionSpec as P

MESH = pl.DeviceIdType.MESH
RELAX = 0.05
CAP = 4
VMEM_LIMIT = 60 * 1024 * 1024
F32 = jnp.float32
BF16 = jnp.bfloat16


def iota(shape, dim):
    return lax.broadcasted_iota(jnp.int32, shape, dim)


def split3(v):
    hi = v.astype(BF16)
    rest = v - hi.astype(F32)
    mid = rest.astype(BF16)
    lo = (rest - mid.astype(F32)).astype(BF16)
    return hi, mid, lo


def inverse_parts(z, n):
    lanes = z.shape[1]
    lane = iota(z.shape, 1)
    w = 1.0 / z
    one = jnp.ones_like(z)
    m = (one, w, one, 1.0 + w)
    step = 1
    while step < n:
        first = lane < step
        b = [jnp.where(first, float(k in (0, 3)), pltpu.roll(v, step, 1)) for k, v in enumerate(m)]
        a = m
        m = (
            a[0] * b[0] + a[1] * b[2],
            a[0] * b[1] + a[1] * b[3],
            a[2] * b[0] + a[3] * b[2],
            a[2] * b[1] + a[3] * b[3],
        )
        step *= 2
    p_next = m[0] + m[1]
    p = jnp.where(lane == 0, 1.0, pltpu.roll(p_next, 1, 1))
    t = jnp.where(lane < n, 1.0 / (z * p * p_next), 0.0)
    p, t = p[:1], t[:1]
    r, c = iota((lanes, lanes), 0), iota((lanes, lanes), 1)
    p_col = jnp.sum(jnp.where(r == c, p, 0.0), axis=1, keepdims=True)
    tail_col = jnp.sum(jnp.where(c >= r, t, 0.0), axis=1, keepdims=True)
    return p_col, tail_col


def kernel(
    dims,
    node_ref, classes_ref, table_ref, z_ref, dest_ref, slot_ref, vec_ref, out_ref,
    fin, xs, ext, fld, pq_send, pq_recv, cols,
    ma_send, ma_recv, mb_recv, sa_send, sa_recv, sb_send, sb_recv,
    edge_send, edge_recv, side_send, side_recv, coef, cls, vec, z_own, dest_own, slot_own, table,
    load_sem, fin_send_sem, fin_recv_sem, pq_send_sem, pq_recv_sem, out_send_sem, out_recv_sem,
    edge_send_sem, edge_recv_sem, side_send_sem, side_recv_sem, ma_send_sem, ma_recv_sem, mb_send_sem, mb_recv_sem,
    sa_send_sem, sa_recv_sem, sb_send_sem, sb_recv_sem, store_sem,
):
    n_y, line, n_tile, rows, width = dims
    n_sec = n_y * line
    per_row = width // 128
    last = rows + 8
    tops = rows // 8
    sec, t = lax.axis_index("sec"), lax.axis_index("tile")
    y, i = sec // line, sec % line

    def at_line(j):
        return (y * line + j, t)

    def at_y(q):
        return (q * line + i, t)

    def at_tile(s):
        return (sec, s)

    def each_on_line(act):
        half = line // 2
        act((i + half) % line)

        @pl.loop(1, half)
        def _(k):
            act((i + half + k) % line)
            act((i + half - k) % line)

    def each_from_first(act):
        @pl.loop(0, line)
        def _(j):
            @pl.when(j != i)
            def _():
                act(j)

    def send(src, dst, send_sem, recv_sem, device):
        pltpu.make_async_remote_copy(
            src_ref=src, dst_ref=dst, send_sem=send_sem, recv_sem=recv_sem, device_id=device, device_id_type=MESH
        ).start()

    def keep(src, dst, sem):
        pltpu.make_async_copy(src, dst, sem).start()

    def wait_for(ref, sem):
        pltpu.make_async_copy(ref, ref, sem).wait()

    before, after = (t + n_tile - 1) % n_tile, (t + 1) % n_tile

    loads = [
        pltpu.make_async_copy(src, dst, load_sem.at[k])
        for k, (src, dst) in enumerate(
            (
                (dest_ref, dest_own),
                (slot_ref, slot_own),
                (vec_ref, vec),
                (z_ref, z_own),
                (table_ref, table),
                (classes_ref.at[0], cls),
            )
        )
    ]
    for load in loads:
        load.start()
    barrier = pltpu.get_barrier_semaphore()

    def greet(device):
        pl.semaphore_signal(barrier, inc=1, device_id=device, device_id_type=MESH)

    each_on_line(lambda j: greet(at_line(j)))
    for k in range(1, n_y):
        greet(at_y((y + k) % n_y))
    for s in (before, after):
        greet(at_tile(s))
    for k in range(per_row):
        greet((y * line + k * tops, after))
        greet((y * line + k * tops + 1 % tops, before))

    ext[:, :, 0:8, :] = jnp.zeros((2, 2, 8, width), F32)
    ext[:, :, last:, :] = jnp.zeros((2, 2, 8, width), F32)
    coef[:, 0:8, :] = jnp.zeros((4, 8, width), F32)
    coef[:, last:, :] = jnp.zeros((4, 8, width), F32)

    on_top = i % tops == 0
    on_bottom = i % tops == 1 % tops
    edges = on_top.astype(jnp.int32) + on_bottom.astype(jnp.int32)
    pl.semaphore_wait(barrier, line - 1 + n_y - 1 + 2 + line * edges)

    def piece(field, j, base):
        top = pl.multiple_of(base + (tops - j % tops) % tops * 8, 8)
        left = pl.multiple_of(j // tops * 128, 128)
        return field.at[pl.ds(top, 8), pl.ds(left, 128)]

    def send_in(field, r, c):
        sems = fin_send_sem.at[r, c], fin_recv_sem.at[r, c]
        each_on_line(lambda j: send(piece(field, j, 0), fin.at[r, c, i], *sems, at_line(j)))
        keep(piece(field, i, 0), fin.at[r, c, i], sems[1])

    for c in range(2):
        send_in(node_ref.at[0, c], 0, c)

    loads[0].wait()
    loads[1].wait()
    dest, slot = dest_own[...], slot_own[...]
    matches = dest.shape[1]
    hot = (iota((n_sec, matches), 0) == dest).astype(F32)
    earlier = (iota((matches, matches), 0) < iota((matches, matches), 1)).astype(F32).astype(BF16)
    hits = jnp.dot(hot.astype(BF16), earlier, preferred_element_type=F32)
    rank = jnp.sum(hot * hits, axis=0, keepdims=True).astype(jnp.int32)
    spot = (slot % per_row) * rows + slot // per_row
    group = 128 // (CAP * n_y)
    base = CAP * n_y * (i % group) + CAP * y + rank
    marks = jnp.where(iota((128, matches), 0) == base, (spot + 1).astype(F32), 0.0)
    sa_send[...] = lax.dot_general(
        hot.astype(BF16), marks.astype(BF16), (((1,), (1,)), ((), ())), preferred_element_type=F32
    ).reshape(n_y, line, 128)
    position = dest * CAP + rank
    loads[2].wait()
    vectors = jnp.concatenate(split3(vec[...]), axis=1)
    for k in range(n_y):
        q = (y + k) % n_y
        place = (iota((line * CAP, matches), 0) + q * (line * CAP) == position).astype(F32).astype(BF16)
        packed = jnp.dot(place, vectors, preferred_element_type=F32)
        packed = (packed[:, :256] + packed[:, 256:512]) + packed[:, 512:]
        for c in range(2):
            ma_send[c, q] = packed[:, c * 128 : c * 128 + 128].reshape(line, CAP, 128)
            if k == 0:
                keep(ma_send.at[c, q], ma_recv.at[c, y], ma_recv_sem.at[c])
            else:
                send(ma_send.at[c, q], ma_recv.at[c, y], ma_send_sem.at[c], ma_recv_sem.at[c], at_y(q))
        if k == 0:
            keep(sa_send.at[q], sa_recv.at[y], sa_recv_sem)
        else:
            send(sa_send.at[q], sa_recv.at[y], sa_send_sem, sa_recv_sem, at_y(q))

    loads[3].wait()
    p_col, tail_col = inverse_parts(jnp.broadcast_to(z_own[...], (8, 128)), n_sec)
    pt_col = p_col * tail_col
    p_own, pt_own = p_col[:line], pt_col[:line]
    for q in range(1, n_y):
        cut = slice(q * line, (q + 1) * line)
        p_own, pt_own = jnp.where(y == q, p_col[cut], p_own), jnp.where(y == q, pt_col[cut], pt_own)
    cols[0] = jnp.broadcast_to(p_own, (line, 128))
    cols[1] = jnp.broadcast_to(pt_own, (line, 128))

    loads[4].wait()
    loads[5].wait()
    classes = cls[...]
    stiffness = jnp.zeros((rows, width), F32)
    for level in range(table.shape[0]):
        stiffness = jnp.where(classes == level, table[level], stiffness)
    coef[0, 8:last, :] = RELAX * stiffness

    def forward_slots():
        wait_for(sa_recv, sa_recv_sem)
        marked = jnp.sum(sa_recv[...], axis=0)
        for j in range(line):
            sb_send[j] = marked[j : j + 1]
        each_on_line(lambda j: send(sb_send.at[j], sb_recv.at[i], sb_send_sem, sb_recv_sem, at_line(j)))
        keep(sb_send.at[i], sb_recv.at[i], sb_recv_sem)

    def forward_matches(c):
        wait_for(ma_recv.at[c], ma_recv_sem.at[c])
        each_on_line(
            lambda j: send(ma_recv.at[c, :, j], mb_recv.at[c, i], mb_send_sem.at[c], mb_recv_sem.at[c], at_line(j))
        )
        keep(ma_recv.at[c, :, i], mb_recv.at[c, i], mb_recv_sem.at[c])

    spots, total = rows * per_row, line * n_y * CAP

    def choose():
        wait_for(sb_recv, sb_recv_sem)
        used = min(group, line)
        chunks = []
        for g in range(line // used):
            part = jnp.sum(jnp.sum(sb_recv[used * g : used * (g + 1)], axis=0), axis=0, keepdims=True)
            chunks.append(part[:, : used * n_y * CAP])
        ids = jnp.concatenate(chunks, axis=1).astype(jnp.int32) - 1
        chosen = (iota((spots, total), 0) == ids).astype(F32)
        counts = jnp.broadcast_to(jnp.sum(chosen, axis=1, keepdims=True), (spots, 128))
        for b in range(per_row):
            lanes = slice(b * 128, (b + 1) * 128)
            coef[1, 8:last, lanes] = (
                1.0 - 4.0 * coef[0, 8:last, lanes] - RELAX * counts[b * rows : (b + 1) * rows]
            )
        return chosen.astype(BF16)

    def place_matches(c, chosen):
        wait_for(mb_recv.at[c], mb_recv_sem.at[c])
        rhs = jnp.concatenate(split3(mb_recv[c].reshape(total, 128)), axis=1)
        sums = jnp.dot(chosen, rhs, preferred_element_type=F32)
        pulled = RELAX * ((sums[:, :128] + sums[:, 128:256]) + sums[:, 256:])
        for b in range(per_row):
            coef[2 + c, 8:last, b * 128 : (b + 1) * 128] = pulled[b * rows : (b + 1) * rows]

    def totals(r, c):
        wait_for(fin.at[r, c], fin_recv_sem.at[r, c])
        low, high = jnp.zeros((8, 128), F32), jnp.zeros((8, 128), F32)
        for j in range(line):
            f = fin[r, c, j]
            low, high = low + cols[0, j : j + 1] * f, high + cols[1, j : j + 1] * f
        pq_send[r, c, 0], pq_send[r, c, 1] = low, high
        sems = pq_send_sem.at[r, c], pq_recv_sem.at[r, c]
        for k in range(1, n_y):
            send(pq_send.at[r, c], pq_recv.at[r, c, y], *sems, at_y((y + k) % n_y))
        keep(pq_send.at[r, c], pq_recv.at[r, c, y], sems[1])

    def solve(r, c):
        wait_for(pq_recv.at[r, c], pq_recv_sem.at[r, c])
        low, high = jnp.zeros((8, 128), F32), jnp.zeros((8, 128), F32)
        for q in range(n_y):
            low = low + jnp.where(q < y, pq_recv[r, c, q, 0], 0.0)
            high = high + jnp.where(q > y, pq_recv[r, c, q, 1], 0.0)
        for j in range(line):
            low = low + cols[0, j : j + 1] * fin[r, c, j]
            xs[r, c, j] = cols[1, j : j + 1] * low
        for j in reversed(range(line)):
            xs[r, c, j] = xs[r, c, j] + cols[0, j : j + 1] * high
            high = high + cols[1, j : j + 1] * fin[r, c, j]
        spot_there = piece(ext.at[r, c], i, 8)
        sems = out_send_sem.at[r, c], out_recv_sem.at[r, c]
        for side, here in ((0, on_top), (1, on_bottom)):

            @pl.when(here)
            def _():
                for j in range(line):
                    edge_send[r, c, side, j] = xs[r, c, j, 6 * side : 6 * side + 2]

        def over(j, side, beyond):
            send(
                edge_send.at[r, c, side, j], edge_recv.at[r, c, side, i // tops],
                edge_send_sem.at[r, c, side], edge_recv_sem.at[r, c, side], (y * line + j, beyond),
            )

        def both(j):
            for side, here, beyond in ((0, on_top, before), (1, on_bottom, after)):

                @pl.when(here)
                def _():
                    over(j, side, beyond)

            send(xs.at[r, c, j], spot_there, *sems, at_line(j))

        order = each_from_first if (r, c) in ((1, 1),) else each_on_line
        order(both)
        for side, here, beyond in ((0, on_top, before), (1, on_bottom, after)):

            @pl.when(here)
            def _():
                over(i, side, beyond)

        keep(xs.at[r, c, i], spot_there, sems[1])

    def send_sides(c):
        which = [2, 0, 1] if c == 0 else [3]
        for side, other, edge in ((0, before, 8), (1, after, last - 1)):
            for k, w in enumerate(which):
                side_send[c, side, k : k + 1, :] = coef[w, edge : edge + 1, :]
            send(
                side_send.at[c, side], side_recv.at[c, side], side_send_sem.at[c], side_recv_sem.at[c], at_tile(other)
            )

    def relax(r, c):
        if r == 0:
            wait_for(side_recv.at[c], side_recv_sem.at[c])
            above = jnp.where(t > 0, side_recv[c, 1], 0.0)
            below = jnp.where(t < n_tile - 1, side_recv[c, 0], 0.0)
            for k, w in enumerate([2, 0, 1] if c == 0 else [3]):
                coef[w, 7:8, :] = above[k : k + 1]
                coef[w, last : last + 1, :] = below[k : k + 1]
        for side in range(2):
            wait_for(edge_recv.at[r, c, side], edge_recv_sem.at[r, c, side])
        for b in range(per_row):
            lanes = slice(b * 128, (b + 1) * 128)
            ext[r, c, 6:8, lanes] = jnp.where(t > 0, edge_recv[r, c, 1, b], 0.0)
            ext[r, c, last : last + 2, lanes] = jnp.where(t < n_tile - 1, edge_recv[r, c, 0, b], 0.0)
        wait_for(ext.at[r, c, pl.ds(8, rows)], out_recv_sem.at[r, c])
        height = rows + 16
        column = iota((height, width), 1)
        v = ext[r, c]
        for _ in range(2):
            left = jnp.where(column == 0, 0.0, pltpu.roll(v, 1, 1))
            right = jnp.where(column == width - 1, 0.0, pltpu.roll(v, width - 1, 1))
            around = (pltpu.roll(v, 1, 0) + pltpu.roll(v, height - 1, 0)) + (left + right)
            v = coef[1] * v + (coef[0] * around + coef[2 + c])
        fld[r, c] = v[8:last]

    forward_matches(0)
    forward_slots()
    totals(0, 0)
    totals(0, 1)
    solve(0, 0)
    forward_matches(1)
    solve(0, 1)
    chosen = choose()
    place_matches(0, chosen)
    send_sides(0)
    relax(0, 0)
    send_in(fld.at[0, 0], 1, 0)
    place_matches(1, chosen)
    send_sides(1)
    relax(0, 1)
    send_in(fld.at[0, 1], 1, 1)
    totals(1, 0)
    solve(1, 0)
    totals(1, 1)
    solve(1, 1)
    for c in range(2):
        relax(1, c)
        keep(fld.at[1, c], out_ref.at[0, c], store_sem.at[c])

    for c in range(2):
        for r in range(2):
            wait_for(fin.at[r, c, pl.ds(0, line - 1)], fin_send_sem.at[r, c])
            wait_for(xs.at[r, c, pl.ds(0, line - 1)], out_send_sem.at[r, c])
            wait_for(pq_recv.at[r, c, pl.ds(0, n_y - 1)], pq_send_sem.at[r, c])
            for side, here in ((0, on_top), (1, on_bottom)):

                @pl.when(here)
                def _():
                    wait_for(edge_send.at[r, c, side], edge_send_sem.at[r, c, side])

        wait_for(ma_send.at[c, pl.ds(0, n_y - 1)], ma_send_sem.at[c])
        wait_for(mb_recv.at[c, pl.ds(0, line - 1)], mb_send_sem.at[c])
        wait_for(side_send.at[c], side_send_sem.at[c])
    wait_for(sa_send.at[pl.ds(0, n_y - 1)], sa_send_sem)
    wait_for(sb_recv.at[pl.ds(0, line - 1)], sb_send_sem)
    for c in range(2):
        pltpu.make_async_copy(fld.at[1, c], out_ref.at[0, c], store_sem.at[c]).wait()


def local(n_sec, n_tile, node_flow, classes, table, z_couple, match_dest, match_slot, match_vectors):
    _, comps, rows, width = node_flow.shape
    line = rows * width // 1024
    n_y = n_sec // line
    matches = match_vectors.shape[0]
    vmem, dma = pltpu.VMEM, pltpu.SemaphoreType.DMA
    z = jnp.pad(z_couple, (0, 128 - n_sec), constant_values=26.0).reshape(1, 128)
    return pl.pallas_call(
        functools.partial(kernel, (n_y, line, n_tile, rows, width)),
        out_shape=jax.ShapeDtypeStruct(node_flow.shape, F32),
        in_specs=[pl.BlockSpec(memory_space=pl.ANY)] * 7,
        out_specs=pl.BlockSpec(memory_space=pl.ANY),
        scratch_shapes=[
            vmem((2, 2, line, 8, 128), F32),
            vmem((2, 2, line, 8, 128), F32),
            vmem((2, 2, rows + 16, width), F32),
            vmem((2, 2, rows, width), F32),
            vmem((2, 2, 2, 8, 128), F32),
            vmem((2, 2, n_y, 2, 8, 128), F32),
            vmem((2, line, 128), F32),
            vmem((2, n_y, line, CAP, 128), F32),
            vmem((2, n_y, line, CAP, 128), F32),
            vmem((2, line, n_y, CAP, 128), F32),
            vmem((n_y, line, 128), F32),
            vmem((n_y, line, 128), F32),
            vmem((line, 1, 128), F32),
            vmem((line, 1, 128), F32),
            vmem((2, 2, 2, line, 2, 128), F32),
            vmem((2, 2, 2, width // 128, 2, 128), F32),
            vmem((2, 2, 8, width), F32),
            vmem((2, 2, 8, width), F32),
            vmem((4, rows + 16, width), F32),
            vmem((rows, width), jnp.int32),
            vmem((matches, 256), F32),
            vmem((1, 128), F32),
            vmem((1, matches), jnp.int32),
            vmem((1, matches), jnp.int32),
            pltpu.SMEM((table.shape[0],), F32),
            dma((6,)),
            *([dma((2, 2))] * 6),
            *([dma((2, 2, 2))] * 2),
            *([dma((2,))] * 6),
            *([dma(())] * 4),
            dma((2,)),
        ],
        compiler_params=pltpu.CompilerParams(
            collective_id=0, has_side_effects=True, vmem_limit_bytes=VMEM_LIMIT
        ),
        cost_estimate=pl.CostEstimate(flops=10**9, bytes_accessed=10**6, transcendentals=0),
        name="align",
    )(
        node_flow,
        classes,
        table,
        z,
        match_dest.reshape(1, matches),
        match_slot.reshape(1, matches),
        match_vectors,
    )


def solution(mesh):
    return jax.shard_map(
        functools.partial(local, mesh.shape["sec"], mesh.shape["tile"]),
        mesh=mesh,
        in_specs=(
            P("sec", None, "tile", None),
            P("sec", "tile", None),
            P(),
            P(),
            P(("sec", "tile"), None),
            P(("sec", "tile")),
            P(("sec", "tile"), None),
        ),
        out_specs=P("sec", None, "tile", None),
        check_vma=False,
    )
```

```python
import functools

import jax
import jax.numpy as jnp
from jax import lax
from jax.experimental import pallas as pl
from jax.experimental.pallas import tpu as pltpu
from jax.sharding import PartitionSpec as P

MESH = pl.DeviceIdType.MESH
RELAX = 0.05
CAP = 4
VMEM_LIMIT = 60 * 1024 * 1024
F32 = jnp.float32
BF16 = jnp.bfloat16


def iota(shape, dim):
    return lax.broadcasted_iota(jnp.int32, shape, dim)


def split3(v):
    hi = v.astype(BF16)
    rest = v - hi.astype(F32)
    mid = rest.astype(BF16)
    lo = (rest - mid.astype(F32)).astype(BF16)
    return hi, mid, lo


def inverse_parts(z, n):
    lanes = z.shape[1]
    lane = iota(z.shape, 1)
    w = 1.0 / z
    one = jnp.ones_like(z)
    m = (one, w, one, 1.0 + w)
    step = 1
    while step < n:
        first = lane < step
        b = [jnp.where(first, float(k in (0, 3)), pltpu.roll(v, step, 1)) for k, v in enumerate(m)]
        a = m
        m = (
            a[0] * b[0] + a[1] * b[2],
            a[0] * b[1] + a[1] * b[3],
            a[2] * b[0] + a[3] * b[2],
            a[2] * b[1] + a[3] * b[3],
        )
        step *= 2
    p_next = m[0] + m[1]
    p = jnp.where(lane == 0, 1.0, pltpu.roll(p_next, 1, 1))
    t = jnp.where(lane < n, 1.0 / (z * p * p_next), 0.0)
    p, t = p[:1], t[:1]
    r, c = iota((lanes, lanes), 0), iota((lanes, lanes), 1)
    p_col = jnp.sum(jnp.where(r == c, p, 0.0), axis=1, keepdims=True)
    tail_col = jnp.sum(jnp.where(c >= r, t, 0.0), axis=1, keepdims=True)
    return p_col, tail_col


def kernel(
    dims,
    node_ref, classes_ref, table_ref, z_ref, dest_ref, slot_ref, vec_ref, out_ref,
    fin, xs, ext, fld, pq_send, pq_recv, cols,
    ma_send, ma_recv, mb_recv, sa_send, sa_recv, sb_send, sb_recv,
    edge_send, edge_recv, side_send, side_recv, coef, cls, vec, z_own, dest_own, slot_own, table,
    load_sem, fin_send_sem, fin_recv_sem, pq_send_sem, pq_recv_sem, out_send_sem, out_recv_sem,
    edge_send_sem, edge_recv_sem, side_send_sem, side_recv_sem, ma_send_sem, ma_recv_sem, mb_send_sem, mb_recv_sem,
    sa_send_sem, sa_recv_sem, sb_send_sem, sb_recv_sem, store_sem,
):
    n_y, line, n_tile, rows, width = dims
    n_sec = n_y * line
    per_row = width // 128
    last = rows + 8
    tops = rows // 8
    sec, t = lax.axis_index("sec"), lax.axis_index("tile")
    y, i = sec // line, sec % line

    def at_line(j):
        return (y * line + j, t)

    def at_y(q):
        return (q * line + i, t)

    def at_tile(s):
        return (sec, s)

    def each_on_line(act):
        half = line // 2
        act((i + half) % line)

        @pl.loop(1, half)
        def _(k):
            act((i + half + k) % line)
            act((i + half - k) % line)

    def each_from_first(act):
        @pl.loop(0, line)
        def _(j):
            @pl.when(j != i)
            def _():
                act(j)

    def send(src, dst, send_sem, recv_sem, device):
        pltpu.make_async_remote_copy(
            src_ref=src, dst_ref=dst, send_sem=send_sem, recv_sem=recv_sem, device_id=device, device_id_type=MESH
        ).start()

    def keep(src, dst, sem):
        pltpu.make_async_copy(src, dst, sem).start()

    def wait_for(ref, sem):
        pltpu.make_async_copy(ref, ref, sem).wait()

    before, after = (t + n_tile - 1) % n_tile, (t + 1) % n_tile

    loads = [
        pltpu.make_async_copy(src, dst, load_sem.at[k])
        for k, (src, dst) in enumerate(
            (
                (dest_ref, dest_own),
                (slot_ref, slot_own),
                (vec_ref, vec),
                (z_ref, z_own),
                (table_ref, table),
                (classes_ref.at[0], cls),
            )
        )
    ]
    for load in loads:
        load.start()
    barrier = pltpu.get_barrier_semaphore()

    def greet(device):
        pl.semaphore_signal(barrier, inc=1, device_id=device, device_id_type=MESH)

    each_on_line(lambda j: greet(at_line(j)))
    for k in range(1, n_y):
        greet(at_y((y + k) % n_y))
    for s in (before, after):
        greet(at_tile(s))
    for k in range(per_row):
        greet((y * line + k * tops, after))
        greet((y * line + k * tops + 1 % tops, before))

    ext[:, :, 0:8, :] = jnp.zeros((2, 2, 8, width), F32)
    ext[:, :, last:, :] = jnp.zeros((2, 2, 8, width), F32)
    coef[:, 0:8, :] = jnp.zeros((4, 8, width), F32)
    coef[:, last:, :] = jnp.zeros((4, 8, width), F32)

    on_top = i % tops == 0
    on_bottom = i % tops == 1 % tops
    edges = on_top.astype(jnp.int32) + on_bottom.astype(jnp.int32)
    pl.semaphore_wait(barrier, line - 1 + n_y - 1 + 2 + line * edges)

    def piece(field, j, base):
        top = pl.multiple_of(base + (tops - j % tops) % tops * 8, 8)
        left = pl.multiple_of(j // tops * 128, 128)
        return field.at[pl.ds(top, 8), pl.ds(left, 128)]

    def send_in(field, r, c):
        sems = fin_send_sem.at[r, c], fin_recv_sem.at[r, c]
        each_on_line(lambda j: send(piece(field, j, 0), fin.at[r, c, i], *sems, at_line(j)))
        keep(piece(field, i, 0), fin.at[r, c, i], sems[1])

    for c in range(2):
        send_in(node_ref.at[0, c], 0, c)

    loads[0].wait()
    loads[1].wait()
    dest, slot = dest_own[...], slot_own[...]
    matches = dest.shape[1]
    hot = (iota((n_sec, matches), 0) == dest).astype(F32)
    earlier = (iota((matches, matches), 0) < iota((matches, matches), 1)).astype(F32).astype(BF16)
    hits = jnp.dot(hot.astype(BF16), earlier, preferred_element_type=F32)
    rank = jnp.sum(hot * hits, axis=0, keepdims=True).astype(jnp.int32)
    spot = (slot % per_row) * rows + slot // per_row
    group = 128 // (CAP * n_y)
    base = CAP * n_y * (i % group) + CAP * y + rank
    marks = jnp.where(iota((128, matches), 0) == base, (spot + 1).astype(F32), 0.0)
    sa_send[...] = lax.dot_general(
        hot.astype(BF16), marks.astype(BF16), (((1,), (1,)), ((), ())), preferred_element_type=F32
    ).reshape(n_y, line, 128)
    position = dest * CAP + rank
    loads[2].wait()
    vectors = jnp.concatenate(split3(vec[...]), axis=1)
    for k in range(n_y):
        q = (y + k) % n_y
        place = (iota((line * CAP, matches), 0) + q * (line * CAP) == position).astype(F32).astype(BF16)
        packed = jnp.dot(place, vectors, preferred_element_type=F32)
        packed = (packed[:, :256] + packed[:, 256:512]) + packed[:, 512:]
        for c in range(2):
            ma_send[c, q] = packed[:, c * 128 : c * 128 + 128].reshape(line, CAP, 128)
            if k == 0:
                keep(ma_send.at[c, q], ma_recv.at[c, y], ma_recv_sem.at[c])
            else:
                send(ma_send.at[c, q], ma_recv.at[c, y], ma_send_sem.at[c], ma_recv_sem.at[c], at_y(q))
        if k == 0:
            keep(sa_send.at[q], sa_recv.at[y], sa_recv_sem)
        else:
            send(sa_send.at[q], sa_recv.at[y], sa_send_sem, sa_recv_sem, at_y(q))

    loads[3].wait()
    p_col, tail_col = inverse_parts(jnp.broadcast_to(z_own[...], (8, 128)), n_sec)
    pt_col = p_col * tail_col
    p_own, pt_own = p_col[:line], pt_col[:line]
    for q in range(1, n_y):
        cut = slice(q * line, (q + 1) * line)
        p_own, pt_own = jnp.where(y == q, p_col[cut], p_own), jnp.where(y == q, pt_col[cut], pt_own)
    cols[0] = jnp.broadcast_to(p_own, (line, 128))
    cols[1] = jnp.broadcast_to(pt_own, (line, 128))

    loads[4].wait()
    loads[5].wait()
    classes = cls[...]
    stiffness = jnp.zeros((rows, width), F32)
    for level in range(table.shape[0]):
        stiffness = jnp.where(classes == level, table[level], stiffness)
    coef[0, 8:last, :] = RELAX * stiffness

    def forward_slots():
        wait_for(sa_recv, sa_recv_sem)
        marked = jnp.sum(sa_recv[...], axis=0)
        for j in range(line):
            sb_send[j] = marked[j : j + 1]
        each_on_line(lambda j: send(sb_send.at[j], sb_recv.at[i], sb_send_sem, sb_recv_sem, at_line(j)))
        keep(sb_send.at[i], sb_recv.at[i], sb_recv_sem)

    def forward_matches(c):
        wait_for(ma_recv.at[c], ma_recv_sem.at[c])
        each_on_line(
            lambda j: send(ma_recv.at[c, :, j], mb_recv.at[c, i], mb_send_sem.at[c], mb_recv_sem.at[c], at_line(j))
        )
        keep(ma_recv.at[c, :, i], mb_recv.at[c, i], mb_recv_sem.at[c])

    spots, total = rows * per_row, line * n_y * CAP

    def choose():
        wait_for(sb_recv, sb_recv_sem)
        used = min(group, line)
        chunks = []
        for g in range(line // used):
            part = jnp.sum(jnp.sum(sb_recv[used * g : used * (g + 1)], axis=0), axis=0, keepdims=True)
            chunks.append(part[:, : used * n_y * CAP])
        ids = jnp.concatenate(chunks, axis=1).astype(jnp.int32) - 1
        chosen = (iota((spots, total), 0) == ids).astype(F32)
        counts = jnp.broadcast_to(jnp.sum(chosen, axis=1, keepdims=True), (spots, 128))
        for b in range(per_row):
            lanes = slice(b * 128, (b + 1) * 128)
            coef[1, 8:last, lanes] = (
                1.0 - 4.0 * coef[0, 8:last, lanes] - RELAX * counts[b * rows : (b + 1) * rows]
            )
        return chosen.astype(BF16)

    def place_matches(c, chosen):
        wait_for(mb_recv.at[c], mb_recv_sem.at[c])
        rhs = jnp.concatenate(split3(mb_recv[c].reshape(total, 128)), axis=1)
        sums = jnp.dot(chosen, rhs, preferred_element_type=F32)
        pulled = RELAX * ((sums[:, :128] + sums[:, 128:256]) + sums[:, 256:])
        for b in range(per_row):
            coef[2 + c, 8:last, b * 128 : (b + 1) * 128] = pulled[b * rows : (b + 1) * rows]

    def totals(r, c):
        wait_for(fin.at[r, c], fin_recv_sem.at[r, c])
        low, high = jnp.zeros((8, 128), F32), jnp.zeros((8, 128), F32)
        for j in range(line):
            f = fin[r, c, j]
            low, high = low + cols[0, j : j + 1] * f, high + cols[1, j : j + 1] * f
        pq_send[r, c, 0], pq_send[r, c, 1] = low, high
        sems = pq_send_sem.at[r, c], pq_recv_sem.at[r, c]
        for k in range(1, n_y):
            send(pq_send.at[r, c], pq_recv.at[r, c, y], *sems, at_y((y + k) % n_y))
        keep(pq_send.at[r, c], pq_recv.at[r, c, y], sems[1])

    def solve(r, c):
        wait_for(pq_recv.at[r, c], pq_recv_sem.at[r, c])
        low, high = jnp.zeros((8, 128), F32), jnp.zeros((8, 128), F32)
        for q in range(n_y):
            low = low + jnp.where(q < y, pq_recv[r, c, q, 0], 0.0)
            high = high + jnp.where(q > y, pq_recv[r, c, q, 1], 0.0)
        for j in range(line):
            low = low + cols[0, j : j + 1] * fin[r, c, j]
            xs[r, c, j] = cols[1, j : j + 1] * low
        for j in reversed(range(line)):
            xs[r, c, j] = xs[r, c, j] + cols[0, j : j + 1] * high
            high = high + cols[1, j : j + 1] * fin[r, c, j]
        spot_there = piece(ext.at[r, c], i, 8)
        sems = out_send_sem.at[r, c], out_recv_sem.at[r, c]
        for side, here in ((0, on_top), (1, on_bottom)):

            @pl.when(here)
            def _():
                for j in range(line):
                    edge_send[r, c, side, j] = xs[r, c, j, 6 * side : 6 * side + 2]

        def over(j, side, beyond):
            send(
                edge_send.at[r, c, side, j], edge_recv.at[r, c, side, i // tops],
                edge_send_sem.at[r, c, side], edge_recv_sem.at[r, c, side], (y * line + j, beyond),
            )

        def both(j):
            for side, here, beyond in ((0, on_top, before), (1, on_bottom, after)):

                @pl.when(here)
                def _():
                    over(j, side, beyond)

            send(xs.at[r, c, j], spot_there, *sems, at_line(j))

        order = each_from_first if (r, c) in ((1, 1),) else each_on_line
        order(both)
        for side, here, beyond in ((0, on_top, before), (1, on_bottom, after)):

            @pl.when(here)
            def _():
                over(i, side, beyond)

        keep(xs.at[r, c, i], spot_there, sems[1])

    def send_sides(c):
        which = [2, 0, 1] if c == 0 else [3]
        for side, other, edge in ((0, before, 8), (1, after, last - 1)):
            for k, w in enumerate(which):
                side_send[c, side, k : k + 1, :] = coef[w, edge : edge + 1, :]
            send(
                side_send.at[c, side], side_recv.at[c, side], side_send_sem.at[c], side_recv_sem.at[c], at_tile(other)
            )

    def relax(r, c):
        if r == 0:
            wait_for(side_recv.at[c], side_recv_sem.at[c])
            above = jnp.where(t > 0, side_recv[c, 1], 0.0)
            below = jnp.where(t < n_tile - 1, side_recv[c, 0], 0.0)
            for k, w in enumerate([2, 0, 1] if c == 0 else [3]):
                coef[w, 7:8, :] = above[k : k + 1]
                coef[w, last : last + 1, :] = below[k : k + 1]
        for side in range(2):
            wait_for(edge_recv.at[r, c, side], edge_recv_sem.at[r, c, side])
        for b in range(per_row):
            lanes = slice(b * 128, (b + 1) * 128)
            ext[r, c, 6:8, lanes] = jnp.where(t > 0, edge_recv[r, c, 1, b], 0.0)
            ext[r, c, last : last + 2, lanes] = jnp.where(t < n_tile - 1, edge_recv[r, c, 0, b], 0.0)
        wait_for(ext.at[r, c, pl.ds(8, rows)], out_recv_sem.at[r, c])
        height = rows + 16
        column = iota((height, width), 1)
        v = ext[r, c]
        for _ in range(2):
            left = jnp.where(column == 0, 0.0, pltpu.roll(v, 1, 1))
            right = jnp.where(column == width - 1, 0.0, pltpu.roll(v, width - 1, 1))
            around = (pltpu.roll(v, 1, 0) + pltpu.roll(v, height - 1, 0)) + (left + right)
            v = coef[1] * v + (coef[0] * around + coef[2 + c])
        fld[r, c] = v[8:last]

    forward_matches(0)
    forward_slots()
    forward_matches(1)
    totals(0, 0)
    totals(0, 1)
    solve(0, 0)
    solve(0, 1)
    chosen = choose()
    place_matches(0, chosen)
    send_sides(0)
    relax(0, 0)
    send_in(fld.at[0, 0], 1, 0)
    place_matches(1, chosen)
    send_sides(1)
    relax(0, 1)
    send_in(fld.at[0, 1], 1, 1)
    totals(1, 0)
    solve(1, 0)
    totals(1, 1)
    solve(1, 1)
    for c in range(2):
        relax(1, c)
        keep(fld.at[1, c], out_ref.at[0, c], store_sem.at[c])

    for c in range(2):
        for r in range(2):
            wait_for(fin.at[r, c, pl.ds(0, line - 1)], fin_send_sem.at[r, c])
            wait_for(xs.at[r, c, pl.ds(0, line - 1)], out_send_sem.at[r, c])
            wait_for(pq_recv.at[r, c, pl.ds(0, n_y - 1)], pq_send_sem.at[r, c])
            for side, here in ((0, on_top), (1, on_bottom)):

                @pl.when(here)
                def _():
                    wait_for(edge_send.at[r, c, side], edge_send_sem.at[r, c, side])

        wait_for(ma_send.at[c, pl.ds(0, n_y - 1)], ma_send_sem.at[c])
        wait_for(mb_recv.at[c, pl.ds(0, line - 1)], mb_send_sem.at[c])
        wait_for(side_send.at[c], side_send_sem.at[c])
    wait_for(sa_send.at[pl.ds(0, n_y - 1)], sa_send_sem)
    wait_for(sb_recv.at[pl.ds(0, line - 1)], sb_send_sem)
    for c in range(2):
        pltpu.make_async_copy(fld.at[1, c], out_ref.at[0, c], store_sem.at[c]).wait()


def local(n_sec, n_tile, node_flow, classes, table, z_couple, match_dest, match_slot, match_vectors):
    _, comps, rows, width = node_flow.shape
    line = rows * width // 1024
    n_y = n_sec // line
    matches = match_vectors.shape[0]
    vmem, dma = pltpu.VMEM, pltpu.SemaphoreType.DMA
    z = jnp.pad(z_couple, (0, 128 - n_sec), constant_values=26.0).reshape(1, 128)
    return pl.pallas_call(
        functools.partial(kernel, (n_y, line, n_tile, rows, width)),
        out_shape=jax.ShapeDtypeStruct(node_flow.shape, F32),
        in_specs=[pl.BlockSpec(memory_space=pl.ANY)] * 7,
        out_specs=pl.BlockSpec(memory_space=pl.ANY),
        scratch_shapes=[
            vmem((2, 2, line, 8, 128), F32),
            vmem((2, 2, line, 8, 128), F32),
            vmem((2, 2, rows + 16, width), F32),
            vmem((2, 2, rows, width), F32),
            vmem((2, 2, 2, 8, 128), F32),
            vmem((2, 2, n_y, 2, 8, 128), F32),
            vmem((2, line, 128), F32),
            vmem((2, n_y, line, CAP, 128), F32),
            vmem((2, n_y, line, CAP, 128), F32),
            vmem((2, line, n_y, CAP, 128), F32),
            vmem((n_y, line, 128), F32),
            vmem((n_y, line, 128), F32),
            vmem((line, 1, 128), F32),
            vmem((line, 1, 128), F32),
            vmem((2, 2, 2, line, 2, 128), F32),
            vmem((2, 2, 2, width // 128, 2, 128), F32),
            vmem((2, 2, 8, width), F32),
            vmem((2, 2, 8, width), F32),
            vmem((4, rows + 16, width), F32),
            vmem((rows, width), jnp.int32),
            vmem((matches, 256), F32),
            vmem((1, 128), F32),
            vmem((1, matches), jnp.int32),
            vmem((1, matches), jnp.int32),
            pltpu.SMEM((table.shape[0],), F32),
            dma((6,)),
            *([dma((2, 2))] * 6),
            *([dma((2, 2, 2))] * 2),
            *([dma((2,))] * 6),
            *([dma(())] * 4),
            dma((2,)),
        ],
        compiler_params=pltpu.CompilerParams(
            collective_id=0, has_side_effects=True, vmem_limit_bytes=VMEM_LIMIT
        ),
        cost_estimate=pl.CostEstimate(flops=10**9, bytes_accessed=10**6, transcendentals=0),
        name="align",
    )(
        node_flow,
        classes,
        table,
        z,
        match_dest.reshape(1, matches),
        match_slot.reshape(1, matches),
        match_vectors,
    )


def solution(mesh):
    return jax.shard_map(
        functools.partial(local, mesh.shape["sec"], mesh.shape["tile"]),
        mesh=mesh,
        in_specs=(
            P("sec", None, "tile", None),
            P("sec", "tile", None),
            P(),
            P(),
            P(("sec", "tile"), None),
            P(("sec", "tile")),
            P(("sec", "tile"), None),
        ),
        out_specs=P("sec", None, "tile", None),
        check_vma=False,
    )
```

```python
import functools

import jax
import jax.numpy as jnp
from jax import lax
from jax.experimental import pallas as pl
from jax.experimental.pallas import tpu as pltpu
from jax.sharding import PartitionSpec as P

MESH = pl.DeviceIdType.MESH
RELAX = 0.05
CAP = 4
VMEM_LIMIT = 60 * 1024 * 1024
F32 = jnp.float32
BF16 = jnp.bfloat16


def iota(shape, dim):
    return lax.broadcasted_iota(jnp.int32, shape, dim)


def split3(v):
    hi = v.astype(BF16)
    rest = v - hi.astype(F32)
    mid = rest.astype(BF16)
    lo = (rest - mid.astype(F32)).astype(BF16)
    return hi, mid, lo


def inverse_parts(z, n):
    lanes = z.shape[1]
    lane = iota(z.shape, 1)
    w = 1.0 / z
    one = jnp.ones_like(z)
    m = (one, w, one, 1.0 + w)
    step = 1
    while step < n:
        first = lane < step
        b = [jnp.where(first, float(k in (0, 3)), pltpu.roll(v, step, 1)) for k, v in enumerate(m)]
        a = m
        m = (
            a[0] * b[0] + a[1] * b[2],
            a[0] * b[1] + a[1] * b[3],
            a[2] * b[0] + a[3] * b[2],
            a[2] * b[1] + a[3] * b[3],
        )
        step *= 2
    p_next = m[0] + m[1]
    p = jnp.where(lane == 0, 1.0, pltpu.roll(p_next, 1, 1))
    t = jnp.where(lane < n, 1.0 / (z * p * p_next), 0.0)
    p, t = p[:1], t[:1]
    r, c = iota((lanes, lanes), 0), iota((lanes, lanes), 1)
    p_col = jnp.sum(jnp.where(r == c, p, 0.0), axis=1, keepdims=True)
    tail_col = jnp.sum(jnp.where(c >= r, t, 0.0), axis=1, keepdims=True)
    return p_col, tail_col


def kernel(
    dims,
    node_ref, classes_ref, table_ref, z_ref, dest_ref, slot_ref, vec_ref, out_ref,
    fin, xs, ext, fld, pq_send, pq_recv, cols,
    ma_send, ma_recv, mb_recv, sa_send, sa_recv, sb_send, sb_recv,
    edge_send, edge_recv, side_send, side_recv, coef, cls, vec, z_own, dest_own, slot_own, table,
    load_sem, fin_send_sem, fin_recv_sem, pq_send_sem, pq_recv_sem, out_send_sem, out_recv_sem,
    edge_send_sem, edge_recv_sem, side_send_sem, side_recv_sem, ma_send_sem, ma_recv_sem, mb_send_sem, mb_recv_sem,
    sa_send_sem, sa_recv_sem, sb_send_sem, sb_recv_sem, store_sem,
):
    n_y, line, n_tile, rows, width = dims
    n_sec = n_y * line
    per_row = width // 128
    last = rows + 8
    tops = rows // 8
    sec, t = lax.axis_index("sec"), lax.axis_index("tile")
    y, i = sec // line, sec % line

    def at_line(j):
        return (y * line + j, t)

    def at_y(q):
        return (q * line + i, t)

    def at_tile(s):
        return (sec, s)

    def each_on_line(act):
        half = line // 2
        act((i + half) % line)

        @pl.loop(1, half)
        def _(k):
            act((i + half + k) % line)
            act((i + half - k) % line)

    def each_from_first(act):
        @pl.loop(0, line)
        def _(j):
            @pl.when(j != i)
            def _():
                act(j)

    def send(src, dst, send_sem, recv_sem, device):
        pltpu.make_async_remote_copy(
            src_ref=src, dst_ref=dst, send_sem=send_sem, recv_sem=recv_sem, device_id=device, device_id_type=MESH
        ).start()

    def keep(src, dst, sem):
        pltpu.make_async_copy(src, dst, sem).start()

    def wait_for(ref, sem):
        pltpu.make_async_copy(ref, ref, sem).wait()

    before, after = (t + n_tile - 1) % n_tile, (t + 1) % n_tile

    loads = [
        pltpu.make_async_copy(src, dst, load_sem.at[k])
        for k, (src, dst) in enumerate(
            (
                (dest_ref, dest_own),
                (slot_ref, slot_own),
                (vec_ref, vec),
                (z_ref, z_own),
                (table_ref, table),
                (classes_ref.at[0], cls),
            )
        )
    ]
    for load in loads:
        load.start()
    barrier = pltpu.get_barrier_semaphore()

    def greet(device):
        pl.semaphore_signal(barrier, inc=1, device_id=device, device_id_type=MESH)

    each_on_line(lambda j: greet(at_line(j)))
    for k in range(1, n_y):
        greet(at_y((y + k) % n_y))
    for s in (before, after):
        greet(at_tile(s))
    for k in range(per_row):
        greet((y * line + k * tops, after))
        greet((y * line + k * tops + 1 % tops, before))

    ext[:, :, 0:8, :] = jnp.zeros((2, 2, 8, width), F32)
    ext[:, :, last:, :] = jnp.zeros((2, 2, 8, width), F32)
    coef[:, 0:8, :] = jnp.zeros((4, 8, width), F32)
    coef[:, last:, :] = jnp.zeros((4, 8, width), F32)

    on_top = i % tops == 0
    on_bottom = i % tops == 1 % tops
    edges = on_top.astype(jnp.int32) + on_bottom.astype(jnp.int32)
    pl.semaphore_wait(barrier, line - 1 + n_y - 1 + 2 + line * edges)

    def piece(field, j, base):
        top = pl.multiple_of(base + (tops - j % tops) % tops * 8, 8)
        left = pl.multiple_of(j // tops * 128, 128)
        return field.at[pl.ds(top, 8), pl.ds(left, 128)]

    def send_in(field, r, c):
        sems = fin_send_sem.at[r, c], fin_recv_sem.at[r, c]
        each_on_line(lambda j: send(piece(field, j, 0), fin.at[r, c, i], *sems, at_line(j)))
        keep(piece(field, i, 0), fin.at[r, c, i], sems[1])

    for c in range(2):
        send_in(node_ref.at[0, c], 0, c)

    loads[0].wait()
    loads[1].wait()
    dest, slot = dest_own[...], slot_own[...]
    matches = dest.shape[1]
    hot = (iota((n_sec, matches), 0) == dest).astype(F32)
    earlier = (iota((matches, matches), 0) < iota((matches, matches), 1)).astype(F32).astype(BF16)
    hits = jnp.dot(hot.astype(BF16), earlier, preferred_element_type=F32)
    rank = jnp.sum(hot * hits, axis=0, keepdims=True).astype(jnp.int32)
    spot = (slot % per_row) * rows + slot // per_row
    group = 128 // (CAP * n_y)
    base = CAP * n_y * (i % group) + CAP * y + rank
    marks = jnp.where(iota((128, matches), 0) == base, (spot + 1).astype(F32), 0.0)
    sa_send[...] = lax.dot_general(
        hot.astype(BF16), marks.astype(BF16), (((1,), (1,)), ((), ())), preferred_element_type=F32
    ).reshape(n_y, line, 128)
    position = dest * CAP + rank
    loads[2].wait()
    vectors = jnp.concatenate(split3(vec[...]), axis=1)
    for k in range(n_y):
        q = (y + k) % n_y
        place = (iota((line * CAP, matches), 0) + q * (line * CAP) == position).astype(F32).astype(BF16)
        packed = jnp.dot(place, vectors, preferred_element_type=F32)
        packed = (packed[:, :256] + packed[:, 256:512]) + packed[:, 512:]
        for c in range(2):
            ma_send[c, q] = packed[:, c * 128 : c * 128 + 128].reshape(line, CAP, 128)
            if k == 0:
                keep(ma_send.at[c, q], ma_recv.at[c, y], ma_recv_sem.at[c])
            else:
                send(ma_send.at[c, q], ma_recv.at[c, y], ma_send_sem.at[c], ma_recv_sem.at[c], at_y(q))
        if k == 0:
            keep(sa_send.at[q], sa_recv.at[y], sa_recv_sem)
        else:
            send(sa_send.at[q], sa_recv.at[y], sa_send_sem, sa_recv_sem, at_y(q))

    loads[3].wait()
    p_col, tail_col = inverse_parts(jnp.broadcast_to(z_own[...], (8, 128)), n_sec)
    pt_col = p_col * tail_col
    p_own, pt_own = p_col[:line], pt_col[:line]
    for q in range(1, n_y):
        cut = slice(q * line, (q + 1) * line)
        p_own, pt_own = jnp.where(y == q, p_col[cut], p_own), jnp.where(y == q, pt_col[cut], pt_own)
    cols[0] = jnp.broadcast_to(p_own, (line, 128))
    cols[1] = jnp.broadcast_to(pt_own, (line, 128))

    loads[4].wait()
    loads[5].wait()
    classes = cls[...]
    stiffness = jnp.zeros((rows, width), F32)
    for level in range(table.shape[0]):
        stiffness = jnp.where(classes == level, table[level], stiffness)
    coef[0, 8:last, :] = RELAX * stiffness

    def forward_slots():
        wait_for(sa_recv, sa_recv_sem)
        marked = jnp.sum(sa_recv[...], axis=0)
        for j in range(line):
            sb_send[j] = marked[j : j + 1]
        each_on_line(lambda j: send(sb_send.at[j], sb_recv.at[i], sb_send_sem, sb_recv_sem, at_line(j)))
        keep(sb_send.at[i], sb_recv.at[i], sb_recv_sem)

    def forward_matches(c):
        wait_for(ma_recv.at[c], ma_recv_sem.at[c])
        each_on_line(
            lambda j: send(ma_recv.at[c, :, j], mb_recv.at[c, i], mb_send_sem.at[c], mb_recv_sem.at[c], at_line(j))
        )
        keep(ma_recv.at[c, :, i], mb_recv.at[c, i], mb_recv_sem.at[c])

    spots, total = rows * per_row, line * n_y * CAP

    def choose():
        wait_for(sb_recv, sb_recv_sem)
        used = min(group, line)
        chunks = []
        for g in range(line // used):
            part = jnp.sum(jnp.sum(sb_recv[used * g : used * (g + 1)], axis=0), axis=0, keepdims=True)
            chunks.append(part[:, : used * n_y * CAP])
        ids = jnp.concatenate(chunks, axis=1).astype(jnp.int32) - 1
        chosen = (iota((spots, total), 0) == ids).astype(F32)
        counts = jnp.broadcast_to(jnp.sum(chosen, axis=1, keepdims=True), (spots, 128))
        for b in range(per_row):
            lanes = slice(b * 128, (b + 1) * 128)
            coef[1, 8:last, lanes] = (
                1.0 - 4.0 * coef[0, 8:last, lanes] - RELAX * counts[b * rows : (b + 1) * rows]
            )
        return chosen.astype(BF16)

    def place_matches(c, chosen):
        wait_for(mb_recv.at[c], mb_recv_sem.at[c])
        rhs = jnp.concatenate(split3(mb_recv[c].reshape(total, 128)), axis=1)
        sums = jnp.dot(chosen, rhs, preferred_element_type=F32)
        pulled = RELAX * ((sums[:, :128] + sums[:, 128:256]) + sums[:, 256:])
        for b in range(per_row):
            coef[2 + c, 8:last, b * 128 : (b + 1) * 128] = pulled[b * rows : (b + 1) * rows]

    def totals(r, c):
        wait_for(fin.at[r, c], fin_recv_sem.at[r, c])
        low, high = jnp.zeros((8, 128), F32), jnp.zeros((8, 128), F32)
        for j in range(line):
            f = fin[r, c, j]
            low, high = low + cols[0, j : j + 1] * f, high + cols[1, j : j + 1] * f
        pq_send[r, c, 0], pq_send[r, c, 1] = low, high
        sems = pq_send_sem.at[r, c], pq_recv_sem.at[r, c]
        for k in sorted(range(1, n_y), key=lambda k: -min(k, n_y - k)):
            send(pq_send.at[r, c], pq_recv.at[r, c, y], *sems, at_y((y + k) % n_y))
        keep(pq_send.at[r, c], pq_recv.at[r, c, y], sems[1])

    def solve(r, c):
        wait_for(pq_recv.at[r, c], pq_recv_sem.at[r, c])
        low, high = jnp.zeros((8, 128), F32), jnp.zeros((8, 128), F32)
        for q in range(n_y):
            low = low + jnp.where(q < y, pq_recv[r, c, q, 0], 0.0)
            high = high + jnp.where(q > y, pq_recv[r, c, q, 1], 0.0)
        for j in range(line):
            low = low + cols[0, j : j + 1] * fin[r, c, j]
            xs[r, c, j] = cols[1, j : j + 1] * low
        for j in reversed(range(line)):
            xs[r, c, j] = xs[r, c, j] + cols[0, j : j + 1] * high
            high = high + cols[1, j : j + 1] * fin[r, c, j]
        spot_there = piece(ext.at[r, c], i, 8)
        sems = out_send_sem.at[r, c], out_recv_sem.at[r, c]
        for side, here in ((0, on_top), (1, on_bottom)):

            @pl.when(here)
            def _():
                for j in range(line):
                    edge_send[r, c, side, j] = xs[r, c, j, 6 * side : 6 * side + 2]

        def over(j, side, beyond):
            send(
                edge_send.at[r, c, side, j], edge_recv.at[r, c, side, i // tops],
                edge_send_sem.at[r, c, side], edge_recv_sem.at[r, c, side], (y * line + j, beyond),
            )

        def both(j):
            for side, here, beyond in ((0, on_top, before), (1, on_bottom, after)):

                @pl.when(here)
                def _():
                    over(j, side, beyond)

            send(xs.at[r, c, j], spot_there, *sems, at_line(j))

        order = each_from_first if (r, c) in ((1, 1),) else each_on_line
        order(both)
        for side, here, beyond in ((0, on_top, before), (1, on_bottom, after)):

            @pl.when(here)
            def _():
                over(i, side, beyond)

        keep(xs.at[r, c, i], spot_there, sems[1])

    def send_sides(c):
        which = [2, 0, 1] if c == 0 else [3]
        for side, other, edge in ((0, before, 8), (1, after, last - 1)):
            for k, w in enumerate(which):
                side_send[c, side, k : k + 1, :] = coef[w, edge : edge + 1, :]
            send(
                side_send.at[c, side], side_recv.at[c, side], side_send_sem.at[c], side_recv_sem.at[c], at_tile(other)
            )

    def relax(r, c):
        if r == 0:
            wait_for(side_recv.at[c], side_recv_sem.at[c])
            above = jnp.where(t > 0, side_recv[c, 1], 0.0)
            below = jnp.where(t < n_tile - 1, side_recv[c, 0], 0.0)
            for k, w in enumerate([2, 0, 1] if c == 0 else [3]):
                coef[w, 7:8, :] = above[k : k + 1]
                coef[w, last : last + 1, :] = below[k : k + 1]
        for side in range(2):
            wait_for(edge_recv.at[r, c, side], edge_recv_sem.at[r, c, side])
        for b in range(per_row):
            lanes = slice(b * 128, (b + 1) * 128)
            ext[r, c, 6:8, lanes] = jnp.where(t > 0, edge_recv[r, c, 1, b], 0.0)
            ext[r, c, last : last + 2, lanes] = jnp.where(t < n_tile - 1, edge_recv[r, c, 0, b], 0.0)
        wait_for(ext.at[r, c, pl.ds(8, rows)], out_recv_sem.at[r, c])
        height = rows + 16
        column = iota((height, width), 1)
        v = ext[r, c]
        for _ in range(2):
            left = jnp.where(column == 0, 0.0, pltpu.roll(v, 1, 1))
            right = jnp.where(column == width - 1, 0.0, pltpu.roll(v, width - 1, 1))
            around = (pltpu.roll(v, 1, 0) + pltpu.roll(v, height - 1, 0)) + (left + right)
            v = coef[1] * v + (coef[0] * around + coef[2 + c])
        fld[r, c] = v[8:last]

    forward_matches(0)
    forward_slots()
    forward_matches(1)
    totals(0, 0)
    solve(0, 0)
    totals(0, 1)
    solve(0, 1)
    chosen = choose()
    place_matches(0, chosen)
    send_sides(0)
    place_matches(1, chosen)
    send_sides(1)
    relax(0, 0)
    send_in(fld.at[0, 0], 1, 0)
    relax(0, 1)
    send_in(fld.at[0, 1], 1, 1)
    totals(1, 0)
    solve(1, 0)
    totals(1, 1)
    solve(1, 1)
    for c in range(2):
        relax(1, c)
        keep(fld.at[1, c], out_ref.at[0, c], store_sem.at[c])

    for c in range(2):
        for r in range(2):
            wait_for(fin.at[r, c, pl.ds(0, line - 1)], fin_send_sem.at[r, c])
            wait_for(xs.at[r, c, pl.ds(0, line - 1)], out_send_sem.at[r, c])
            wait_for(pq_recv.at[r, c, pl.ds(0, n_y - 1)], pq_send_sem.at[r, c])
            for side, here in ((0, on_top), (1, on_bottom)):

                @pl.when(here)
                def _():
                    wait_for(edge_send.at[r, c, side], edge_send_sem.at[r, c, side])

        wait_for(ma_send.at[c, pl.ds(0, n_y - 1)], ma_send_sem.at[c])
        wait_for(mb_recv.at[c, pl.ds(0, line - 1)], mb_send_sem.at[c])
        wait_for(side_send.at[c], side_send_sem.at[c])
    wait_for(sa_send.at[pl.ds(0, n_y - 1)], sa_send_sem)
    wait_for(sb_recv.at[pl.ds(0, line - 1)], sb_send_sem)
    for c in range(2):
        pltpu.make_async_copy(fld.at[1, c], out_ref.at[0, c], store_sem.at[c]).wait()


def local(n_sec, n_tile, node_flow, classes, table, z_couple, match_dest, match_slot, match_vectors):
    _, comps, rows, width = node_flow.shape
    line = rows * width // 1024
    n_y = n_sec // line
    matches = match_vectors.shape[0]
    vmem, dma = pltpu.VMEM, pltpu.SemaphoreType.DMA
    z = jnp.pad(z_couple, (0, 128 - n_sec), constant_values=26.0).reshape(1, 128)
    return pl.pallas_call(
        functools.partial(kernel, (n_y, line, n_tile, rows, width)),
        out_shape=jax.ShapeDtypeStruct(node_flow.shape, F32),
        in_specs=[pl.BlockSpec(memory_space=pl.ANY)] * 7,
        out_specs=pl.BlockSpec(memory_space=pl.ANY),
        scratch_shapes=[
            vmem((2, 2, line, 8, 128), F32),
            vmem((2, 2, line, 8, 128), F32),
            vmem((2, 2, rows + 16, width), F32),
            vmem((2, 2, rows, width), F32),
            vmem((2, 2, 2, 8, 128), F32),
            vmem((2, 2, n_y, 2, 8, 128), F32),
            vmem((2, line, 128), F32),
            vmem((2, n_y, line, CAP, 128), F32),
            vmem((2, n_y, line, CAP, 128), F32),
            vmem((2, line, n_y, CAP, 128), F32),
            vmem((n_y, line, 128), F32),
            vmem((n_y, line, 128), F32),
            vmem((line, 1, 128), F32),
            vmem((line, 1, 128), F32),
            vmem((2, 2, 2, line, 2, 128), F32),
            vmem((2, 2, 2, width // 128, 2, 128), F32),
            vmem((2, 2, 8, width), F32),
            vmem((2, 2, 8, width), F32),
            vmem((4, rows + 16, width), F32),
            vmem((rows, width), jnp.int32),
            vmem((matches, 256), F32),
            vmem((1, 128), F32),
            vmem((1, matches), jnp.int32),
            vmem((1, matches), jnp.int32),
            pltpu.SMEM((table.shape[0],), F32),
            dma((6,)),
            *([dma((2, 2))] * 6),
            *([dma((2, 2, 2))] * 2),
            *([dma((2,))] * 6),
            *([dma(())] * 4),
            dma((2,)),
        ],
        compiler_params=pltpu.CompilerParams(
            collective_id=0, has_side_effects=True, vmem_limit_bytes=VMEM_LIMIT
        ),
        cost_estimate=pl.CostEstimate(flops=10**9, bytes_accessed=10**6, transcendentals=0),
        name="align",
    )(
        node_flow,
        classes,
        table,
        z,
        match_dest.reshape(1, matches),
        match_slot.reshape(1, matches),
        match_vectors,
    )


def solution(mesh):
    return jax.shard_map(
        functools.partial(local, mesh.shape["sec"], mesh.shape["tile"]),
        mesh=mesh,
        in_specs=(
            P("sec", None, "tile", None),
            P("sec", "tile", None),
            P(),
            P(),
            P(("sec", "tile"), None),
            P(("sec", "tile")),
            P(("sec", "tile"), None),
        ),
        out_specs=P("sec", None, "tile", None),
        check_vma=False,
    )
```
